32 devices in a mesh: gx: 4 (over x, core), gy: 8 (over z, y).
Axes of the slice: x: 2, y: 2, z: 4, core: 2. Of those that a mesh axis runs over, the one named last changes fastest.
Arguments:
- start_disp: float32 [3, 128, 256, 128], P(None, 'gx', 'gy'), may hold values from -6 to 6
- start_vel: float32 [3, 128, 256, 128], P(None, 'gx', 'gy'), may hold values from -6 to 6
- stiffness: float32 [128, 256, 128], P('gx', 'gy'), may hold values from 0.5 to 2
- cell_mass: float32 [128, 256, 128], P('gx', 'gy'), may hold values from 0.5 to 2
- contact_cells: int32 [4, 8, 512], P('gx', 'gy'), may hold values from 0 to 1023
- contact_match: int32 [4, 8, 512], P('gx', 'gy'), may hold values from 0 to 511, each once within a row
- eroded_cells: int32 [8, 4, 8, 512], P(None, 'gx', 'gy'), may hold values from 0 to 131071
- owner_ids: int32 [8, 4, 8, 512, 1], P(None, 'gx', 'gy'), may hold values from 0 to 7; in each aligned block of 512 rows (0 to 511, 512 to 1023, ..., all dimensions but the last counted through in order) at most 128 rows name the same one
- bed_position: float32 [4, 8, 3, 1024], P('gx', 'gy'), may hold values from -6 to 6
- bed_velocity: float32 [4, 8, 3, 1024], P('gx', 'gy'), may hold values from -6 to 6
- bed_neighbours: int32 [4, 8, 8, 1024], P('gx', 'gy'), may hold values from 0 to 127
Outputs:
- final_disp: float32 [3, 128, 256, 128], P(None, 'gx', 'gy')
- final_vel: float32 [3, 128, 256, 128], P(None, 'gx', 'gy')
The draws below stay inside these ranges and needn't reach their ends.
Inputs may be any that keep to these rules, and one draw needn't show every extreme that they name: `owner_ids`: in each step, at most 128 records of one block name one owner, and some block names some owner exactly 128 times.
All inputs are finite; a program needn't handle non-finite values.
Results may differ from the reference program's by a relative error of at most 0.0001.
Values sent between devices are 32-bit elements; how exact they have to be, the bound alone decides.
A program may use at most 128 MiB of HBM per device.

```python
import math
import jax
import jax.numpy as jnp
import numpy as np

CX = 32
CY = 32
NZ = 128
STEPS = 8
SEG = 512
ER = 512
CAP = 128
KNB = 8
NX = 128
NY = 256
PART = 1024
BLOCK = 128
N_GX = 4
N_GY = 8


def touch_ends(values, rng, low, high):
    longest = values.shape.index(max(values.shape))
    spots = []
    for shift in (0, 1):
        where = [jax.random.randint(jax.random.fold_in(rng, axis), (), 0, length) for axis, length in enumerate(values.shape)]
        where[longest] = (where[longest] + shift) % values.shape[longest]
        spots.append(tuple(where))
    return values.at[spots[0]].set(low).at[spots[1]].set(high)


def levels(rng, extent, split, smallest, high):
    level = 1.0
    for dim, parts in split:
        heights = jax.random.uniform(jax.random.fold_in(jax.random.fold_in(rng, 6), dim), (parts,), jnp.float32, smallest / len(split), high / len(split))
        level = level * jnp.repeat(jnp.exp(heights), extent[dim] // parts).reshape((-1,) + (1,) * (len(extent) - 1 - dim))
    return level


def shared_out(rng, own, number, rows, amount, top, limit, skew):
    ranking = jax.random.permutation(rng, amount)
    heavy_load, ordinary = shares(amount, rows * top, limit, skew, True), shares(amount, rows * top, limit, skew, False)
    places = jnp.arange(amount)

    def named(lengths, rotation):
        used = int((lengths > 0).sum())
        fixed = max(1, used // 4)
        passed = fixed + (places - fixed + rotation * (used - fixed)) % max(1, amount - fixed)
        return jnp.zeros((amount,), jnp.int32).at[ranking[jnp.where(places < fixed, places, passed)]].set(jnp.asarray(lengths, jnp.int32))

    lengths = jnp.where(number % 4 == 0, named(heavy_load, number // 4), named(ordinary, number - number // 4 - 1))
    mixed = jax.random.permutation(jax.random.fold_in(own, 3), amount)
    giver, receiver = mixed[0:amount // 2 * 2:2], mixed[1:amount // 2 * 2:2]
    slack = jnp.minimum(lengths[giver] - 1, limit - lengths[receiver]) // 2
    slack = jnp.where((giver == ranking[0]) | (receiver == ranking[0]) | (lengths[receiver] == 0), 0, jnp.maximum(slack, 0))
    passed = jax.random.randint(jax.random.fold_in(own, 4), (amount // 2,), 0, 1 << 20) % (slack + 1)
    lengths = lengths.at[giver].add(-passed).at[receiver].add(passed)
    items = jnp.searchsorted(jnp.cumsum(lengths), jnp.arange(rows * top), side="right").astype(jnp.int32)
    table = items.reshape(top, rows).T
    table = table[jax.random.permutation(jax.random.fold_in(own, 1), rows)]
    rotation = jax.random.randint(jax.random.fold_in(own, 2), (rows, 1), 0, top)
    return jnp.take_along_axis(table, (jnp.arange(top)[None, :] + rotation) % top, axis=1)


def shares(amount, total, most, skew, full):
    weights = [(1 << 20) // math.isqrt(grade ** skew) + 1 for grade in range(1, amount + 1)]
    largest = most if full else min(most, max(-(-total // amount), total * weights[0] // sum(weights)))
    least = 1 if total - largest >= amount - 1 else 0
    given, surplus = [largest] + [least] * (amount - 1), total - largest - least * (amount - 1)
    while surplus > 0:
        candidates = [i for i in range(1, amount) if given[i] < largest] or [i for i in range(1, amount) if given[i] < most]
        whole, budget = sum([weights[i] for i in candidates]), surplus
        for i in candidates:
            addition = min(most - given[i], max(1, budget * weights[i] // whole), surplus)
            given[i] = given[i] + addition
            surplus = surplus - addition
    return np.array(given)


def normal_values(rng, shape, deviation, most, split=(), held_as=jnp.bfloat16):
    factor_of = levels(rng, shape, split, -0.22, 0.18) if split else 1.0
    result = jax.random.normal(rng, shape, jnp.float32) * deviation * factor_of
    return jnp.minimum(jnp.maximum(result, -most), most).astype(held_as)


def setup_inputs(seed: int = 0) -> dict:
    key_of = jax.random.split(jax.random.key(seed), 12)
    start_disp = normal_values(key_of[0], (3, NX, NY, NZ), 1.0, 6.0, ((1, 4), (2, 8)), jnp.float32)
    start_vel = normal_values(key_of[1], (3, NX, NY, NZ), 1.0, 6.0, ((1, 4), (2, 8)), jnp.float32)
    stiffness = jnp.clip(jnp.exp(math.log(2.0) - 1.3862944 * jax.random.uniform(key_of[2], (NX, NY, NZ), jnp.float32) ** levels(key_of[2], (NX, NY, NZ), ((0, 4), (1, 8)), -0.2, 0.2)), 0.5, 2.0)
    cell_mass = jnp.clip(jnp.exp(math.log(2.0) - 1.3862944 * jax.random.uniform(key_of[3], (NX, NY, NZ), jnp.float32) ** levels(key_of[3], (NX, NY, NZ), ((0, 4), (1, 8)), -0.2, 0.2)), 0.5, 2.0)
    contact_cells = touch_ends(jax.random.randint(key_of[4], (N_GX, N_GY, SEG), 0, CX * CY), jax.random.fold_in(key_of[4], 1), 0, (CX * CY) - 1).astype(jnp.int32)
    contact_match = jax.vmap(lambda own: jax.random.permutation(own, SEG))(jax.random.split(key_of[5], N_GX * N_GY)).reshape((N_GX, N_GY, SEG)).astype(jnp.int32)
    eroded_cells = touch_ends(jax.random.randint(key_of[6], (STEPS, N_GX, N_GY, ER), 0, CX * CY * NZ), jax.random.fold_in(key_of[6], 1), 0, (CX * CY * NZ) - 1).astype(jnp.int32)
    owner_ids_keys = jax.random.split(jax.random.fold_in(key_of[7], 1), STEPS * N_GX * N_GY * ER // ER)
    owner_ids_turns = jax.random.permutation(jax.random.fold_in(key_of[7], 3), STEPS * N_GX * N_GY * ER // ER)
    owner_ids = jax.vmap(lambda own, number: shared_out(jax.random.fold_in(key_of[7], 2), own, number, ER, N_GY, 1, CAP, 2))(owner_ids_keys, owner_ids_turns).reshape((STEPS, N_GX, N_GY, ER, 1))
    bed_position = normal_values(key_of[8], (N_GX, N_GY, 3, PART), 1.0, 6.0, ((0, 4), (1, 8)), jnp.float32)
    bed_velocity = normal_values(key_of[9], (N_GX, N_GY, 3, PART), 1.0, 6.0, ((0, 4), (1, 8)), jnp.float32)
    bed_neighbours = touch_ends(jax.random.randint(key_of[10], (N_GX, N_GY, KNB, PART), 0, BLOCK), jax.random.fold_in(key_of[10], 1), 0, BLOCK - 1).astype(jnp.int32)
    return {"start_disp": start_disp, "start_vel": start_vel, "stiffness": stiffness, "cell_mass": cell_mass, "contact_cells": contact_cells, "contact_match": contact_match, "eroded_cells": eroded_cells, "owner_ids": owner_ids, "bed_position": bed_position, "bed_velocity": bed_velocity, "bed_neighbours": bed_neighbours}


TIME_STEP = 0.2
CONTACT_K = 0.5
PARTICLE_K = 1.0
DRAG_COEF = 0.5


def to_blocks(field):
    comps = field.shape[0]
    return field.reshape(comps, N_GX, CX, N_GY, CY, NZ).transpose(1, 3, 0, 2, 4, 5).reshape(N_GX, N_GY, comps, CX * CY * NZ)


def from_blocks(blocks):
    comps = blocks.shape[2]
    return blocks.reshape(N_GX, N_GY, comps, CX, CY, NZ).transpose(2, 0, 3, 1, 4, 5).reshape(comps, NX, NY, NZ)


def add_rows(field, where, values):
    return field.at[:, where].add(values)


def reference(start_disp, start_vel, stiffness, cell_mass, contact_cells, contact_match, eroded_cells, owner_ids, bed_position, bed_velocity, bed_neighbours):
    displace = start_disp
    velocity = start_vel
    part_pos = bed_position
    part_vel = bed_velocity
    gx_index = jnp.arange(N_GX, dtype=jnp.int32)[:, None, None]
    gy_index = jnp.arange(N_GY, dtype=jnp.int32)[None, :, None]
    slot_row = jnp.arange(PART, dtype=jnp.int32)
    nbr_rows = (slot_row // BLOCK) * BLOCK + bed_neighbours
    mass_blocks = to_blocks(cell_mass[None])[:, :, 0]
    surf_cells = contact_cells * NZ + (NZ - 1)
    adder = jax.vmap(jax.vmap(add_rows))
    for step_id in range(STEPS):
        padded = jnp.pad(displace, ((0, 0), (1, 1), (1, 1), (1, 1)))
        laplace = padded[:, 2:, 1:-1, 1:-1] + padded[:, :-2, 1:-1, 1:-1] + padded[:, 1:-1, 2:, 1:-1] + padded[:, 1:-1, :-2, 1:-1]
        laplace = laplace + (padded[:, 1:-1, 1:-1, 2:] + padded[:, 1:-1, 1:-1, :-2]) - 6.0 * displace
        internal = stiffness[None] * laplace
        force_blocks = to_blocks(internal)
        disp_blocks = to_blocks(displace)
        vel_blocks = to_blocks(velocity)
        seg_rows = jnp.take_along_axis(disp_blocks, surf_cells[:, :, None, :], axis=3)
        partner = seg_rows[jnp.arange(N_GX) ^ 1]
        facing = jnp.take_along_axis(partner, contact_match[:, :, None, :], axis=3)
        force_blocks = adder(force_blocks, surf_cells, CONTACT_K * (facing - seg_rows))
        cells_now = eroded_cells[step_id]
        owners_now = owner_ids[step_id, :, :, :, 0]
        is_owner = owners_now[..., None] == jnp.arange(N_GY, dtype=jnp.int32)
        counted = jnp.cumsum(is_owner.astype(jnp.int32), axis=2)
        slot_rank = jnp.sum(jnp.where(is_owner, counted, 0), axis=-1) - 1
        slot_id = slot_rank * N_GY + gy_index
        rec_mass = jnp.take_along_axis(mass_blocks, cells_now, axis=2)
        rec_disp = jnp.take_along_axis(disp_blocks, cells_now[:, :, None, :], axis=3)
        rec_mom = rec_mass[:, :, None, :] * jnp.take_along_axis(vel_blocks, cells_now[:, :, None, :], axis=3)
        nbr_cells = nbr_rows[gx_index, owners_now, :, slot_id]
        bed_near = part_pos[gx_index[..., None], owners_now[..., None], :, nbr_cells]
        bed_drift = part_vel[gx_index[..., None], owners_now[..., None], :, nbr_cells]
        offset = bed_near - rec_disp.transpose(0, 1, 3, 2)[:, :, :, None, :]
        weights = 1.0 / (1.0 + jnp.sum(offset * offset, axis=-1))
        mass_col = rec_mass[:, :, :, None, None]
        mom_col = rec_mom.transpose(0, 1, 3, 2)[:, :, :, None, :]
        spring = weights[..., None] * (PARTICLE_K * mass_col * offset)
        terms = spring + weights[..., None] * (DRAG_COEF * (mass_col * bed_drift - mom_col))
        rec_force = jnp.sum(terms, axis=3) / KNB
        force_blocks = adder(force_blocks, cells_now, rec_force.transpose(0, 1, 3, 2))
        part_vel = part_vel.at[gx_index[..., None], owners_now[..., None], :, nbr_cells].add(-TIME_STEP * spring / KNB)
        part_pos = part_pos + TIME_STEP * part_vel
        forces = from_blocks(force_blocks)
        velocity = velocity + TIME_STEP * (forces / cell_mass[None])
        displace = displace + TIME_STEP * velocity
    return displace, velocity
```

```python
import functools

import jax
import jax.numpy as jnp
from jax import lax
from jax.experimental import pallas as pl
from jax.experimental.pallas import tpu as pltpu
from jax.sharding import PartitionSpec as P

TIME_STEP = 0.2
CONTACT_K = 0.5
PARTICLE_K = 1.0
DRAG_COEF = 0.5
LANES = 128
F32 = jnp.float32
BF16 = jnp.bfloat16
MESH = pl.DeviceIdType.MESH


def take_lanes(x, idx):
    return jnp.take_along_axis(x, idx, axis=1, mode="promise_in_bounds")


def dot_nt(a, b):
    return lax.dot_general(a, b, (((1,), (1,)), ((), ())), preferred_element_type=F32)


def two_parts(x):
    hi = x.astype(BF16).astype(F32)
    return hi, x - hi


def rows8(row):
    return jnp.broadcast_to(row, (8, row.shape[1]))


def kernel(
    dims,
    cells_s, contact_s, disp_in, vel_in, stiff_in, mass_in, contact_v, match_v, cells_v, owner_v, bpos, bvel, bnbr,
    disp_out, vel_out,
    D, V, A, G, top_add, ye, yh, xh, msg, rx, ans, ax, seg, ps, inv, rank, part, nbr, nbr_hot, seg_hot, b_hi, b_lo,
    out_sem, ye_send, yh_recv, xe_send, xh_recv, m_send, m_recv, a_send, a_recv, p_send, p_recv,
):
    n_gx, n_gy, cx, cy, steps, n_rec, n_seg, n_blocks, n_nbr = dims
    n_cols = cx * cy
    group = LANES // n_gy
    rec_tiles = n_rec // LANES
    seg_tiles = n_seg // LANES
    chunk_x = 8
    chunk = chunk_x * cy
    a = lax.axis_index("gx")
    b = lax.axis_index("gy")
    mate = a + 1 - 2 * lax.rem(a, 2)
    lane = lax.broadcasted_iota(jnp.int32, (8, LANES), 1)
    sub = lax.broadcasted_iota(jnp.int32, (8, LANES), 0)

    flat = G.reshape(n_cols * 8, LANES)

    yh[...] = jnp.zeros_like(yh)
    xh[...] = jnp.zeros_like(xh)

    def init_chunk(i, _):
        x0 = i * chunk_x
        xs = pl.ds(x0, chunk_x)
        m = mass_in[xs].reshape(chunk, LANES)
        A[xs] = TIME_STEP * stiff_in[xs] / mass_in[xs]
        base = pl.multiple_of(i * (chunk * 8), chunk * 8)
        for f in range(3):
            d = disp_in[f, xs]
            v = vel_in[f, xs]
            D[f, pl.ds(x0 + 1, chunk_x)] = d
            V[f, xs] = v
            flat[pl.ds(base + f, chunk, stride=8), :] = d.reshape(chunk, LANES)
            flat[pl.ds(base + 3 + f, chunk, stride=8), :] = v.reshape(chunk, LANES)
            for xx in range(chunk_x):
                ye[0, f, pl.ds(x0 + xx, 1), :] = d[xx, 0:1]
                ye[1, f, pl.ds(x0 + xx, 1), :] = d[xx, cy - 1:cy]
        flat[pl.ds(base + 6, chunk, stride=8), :] = m
        flat[pl.ds(base + 7, chunk, stride=8), :] = jnp.zeros_like(m)
        cols = lax.broadcasted_iota(jnp.int32, (chunk, n_seg), 0) + i * chunk
        seg_hot[pl.ds(pl.multiple_of(i * chunk, chunk), chunk), :] = jnp.where(cols == contact_v[...], 1.0, 0.0).astype(BF16)
        return 0

    lax.fori_loop(0, cx // chunk_x, init_chunk, 0)

    tri = jnp.where(
        lax.broadcasted_iota(jnp.int32, (n_rec, n_rec), 1) <= lax.broadcasted_iota(jnp.int32, (n_rec, n_rec), 0), 1.0, 0.0
    ).astype(BF16)

    def init_step(s, _):
        own = owner_v[pl.ds(s, 1), :]
        mine = lax.broadcasted_iota(jnp.int32, (n_gy, n_rec), 0) == own
        hot = jnp.where(mine, 1.0, 0.0)
        counted = dot_nt(jnp.concatenate([hot] * 2, axis=0).astype(BF16), tri)[:n_gy]
        rk = (jnp.sum(hot * counted, axis=0, keepdims=True) - 1.0).astype(jnp.int32)
        rank[pl.ds(s, 1), :] = rk
        rec = lax.broadcasted_iota(jnp.int32, (n_gy, n_rec), 1) + 1
        lo = jnp.where(mine, (rec & 127).astype(F32), 0.0)
        hi = jnp.where(mine, (rec >> 7).astype(F32), 0.0)
        q_hot = jnp.where(lax.broadcasted_iota(jnp.int32, (LANES, n_rec), 0) == rk, 1.0, 0.0).astype(BF16)
        both = dot_nt(jnp.concatenate([lo, hi], axis=0).astype(BF16), q_hot)
        inv[s] = (both[:n_gy] + 128.0 * both[n_gy:]).astype(jnp.int32) - 1
        return 0

    lax.fori_loop(0, steps, init_step, 0)

    perm = lax.rem(lane, group) * n_gy + lane // group
    nrow = lax.broadcasted_iota(jnp.int32, (LANES, LANES), 0)

    def init_block(j, _):
        at = pl.ds(pl.multiple_of(j * LANES, LANES), LANES)
        rows = jnp.concatenate([bpos[:, at], bvel[:, at], jnp.zeros((2, LANES), F32)], axis=0)
        part[j] = take_lanes(rows, perm)
        old = take_lanes(bnbr[:, at], perm)
        new = lax.rem(old, n_gy) * group + old // n_gy
        nbr[j] = new
        for k in range(n_nbr):
            nbr_hot[j, pl.ds(k * LANES, LANES), :] = jnp.where(nrow == new[k:k + 1], 1.0, 0.0).astype(BF16)
        return 0

    lax.fori_loop(0, n_blocks, init_block, 0)

    barrier = pltpu.get_barrier_semaphore()
    for k in range(1, n_gy):
        pl.semaphore_signal(barrier, inc=1, device_id=(a, lax.rem(b + k, n_gy)), device_id_type=MESH)

    @pl.when(a > 0)
    def _():
        pl.semaphore_signal(barrier, inc=1, device_id=(a - 1, b), device_id_type=MESH)

    @pl.when(a < n_gx - 1)
    def _():
        pl.semaphore_signal(barrier, inc=1, device_id=(a + 1, b), device_id_type=MESH)

    near = jnp.where(a > 0, 1, 0) + jnp.where(a < n_gx - 1, 1, 0)
    pl.semaphore_wait(barrier, n_gy - 1 + near)

    def remote(src, dst, send, recv, to):
        return pltpu.make_async_remote_copy(src_ref=src, dst_ref=dst, send_sem=send, recv_sem=recv, device_id=to, device_id_type=MESH)

    def step(s, _):
        p = lax.rem(s, 2)
        halos = (
            (a > 0, remote(D.at[:, 1], xh.at[p, 1], xe_send.at[0], xh_recv.at[p, 1], (a - 1, b)), 0),
            (a < n_gx - 1, remote(D.at[:, cx], xh.at[p, 0], xe_send.at[1], xh_recv.at[p, 0], (a + 1, b)), 1),
        )
        y_halos = (
            (b > 0, remote(ye.at[0], yh.at[p, 1], ye_send.at[0], yh_recv.at[p, 1], (a, b - 1)), 0),
            (b < n_gy - 1, remote(ye.at[1], yh.at[p, 0], ye_send.at[1], yh_recv.at[p, 0], (a, b + 1)), 1),
        )

        def read_tile(scalar, lane_of):
            def body(i, acc):
                for u in range(8):
                    t = i * 8 + u
                    col, z = lane_of(scalar(t))
                    acc = jnp.where(lane == t, take_lanes(G[col], jnp.full((8, LANES), z, jnp.int32)), acc)
                return acc

            return lax.fori_loop(0, LANES // 8, body, jnp.zeros((8, LANES), F32))

        recs = [
            read_tile(lambda t, w=w: cells_s[s, w * LANES + t], lambda c: (c >> 7, c & 127))
            for w in range(rec_tiles)
        ]
        for o in range(n_gy):
            idx = rows8(inv[s, o:o + 1, :])
            out = jnp.zeros((8, LANES), F32)
            for w in range(rec_tiles):
                out = jnp.where((idx >> 7) == w, take_lanes(recs[w], idx & 127), out)
            msg[o] = out
        rx[p, b] = msg[b]
        m_copies = []
        for k in range(1, n_gy):
            o = lax.rem(b + k, n_gy)
            m_copies.append(remote(msg.at[o], rx.at[p, b], m_send.at[k], m_recv.at[p, b], (a, o)))
            m_copies[-1].start()
        for there, copy, _k in halos + y_halos:
            @pl.when(there)
            def _(copy=copy):
                copy.start()

        segs = [
            read_tile(lambda t, w=w: contact_s[0, w * LANES + t], lambda c: (c, LANES - 1)) for w in range(seg_tiles)
        ]
        for w in range(seg_tiles):
            seg[w] = segs[w]
        p_copy = remote(seg, ps.at[p], p_send, p_recv.at[p], (mate, b))
        p_copy.start()

        def wait_from(dst, recv):
            pltpu.make_async_copy(dst, dst, recv).wait()

        @pl.when(a > 0)
        def _():
            wait_from(xh.at[p, 0], xh_recv.at[p, 0])

        @pl.when(a < n_gx - 1)
        def _():
            wait_from(xh.at[p, 1], xh_recv.at[p, 1])

        @pl.when(b > 0)
        def _():
            wait_from(yh.at[p, 0], yh_recv.at[p, 0])

        @pl.when(b < n_gy - 1)
        def _():
            wait_from(yh.at[p, 1], yh_recv.at[p, 1])

        D[:, 0] = xh[p, 0]
        D[:, cx + 1] = xh[p, 1]
        wait_from(ps.at[p], p_recv.at[p])
        c_parts = [[], []]
        for w in range(seg_tiles):
            idx = rows8(match_v[:, w * LANES:(w + 1) * LANES])
            facing = jnp.zeros((8, LANES), F32)
            for u in range(seg_tiles):
                facing = jnp.where((idx >> 7) == u, take_lanes(ps[p, u], idx & 127), facing)
            pull = (TIME_STEP * CONTACT_K) * (facing - segs[w]) / segs[w][6:7]
            hi, lo = two_parts(pull)
            c_parts[0].append(hi)
            c_parts[1].append(lo)
        zero_rows = jnp.zeros((LANES - 8, n_seg), F32)
        c_mats = [jnp.concatenate([jnp.concatenate(part_, axis=1), zero_rows], axis=0).astype(BF16) for part_ in c_parts]

        def top_chunk(i, _):
            at = pl.ds(pl.multiple_of(i * chunk, chunk), chunk)
            hot = seg_hot[at, :]
            top_add[at, :] = dot_nt(hot, c_mats[0]) + dot_nt(hot, c_mats[1])
            return 0

        lax.fori_loop(0, cx // chunk_x, top_chunk, 0)

        row_i = lax.broadcasted_iota(jnp.int32, (cy, LANES), 0)
        lane_i = lax.broadcasted_iota(jnp.int32, (cy, LANES), 1)

        def lap_row(x, _):
            top = top_add[pl.ds(pl.multiple_of(x * cy, cy), cy), :]
            scale = A[x]
            for f in range(3):
                c = D[f, x + 1]
                lap = D[f, x] + D[f, x + 2] - 6.0 * c
                lap += jnp.where(row_i == 0, yh[p, 0, f, pl.ds(x, 1), :], pltpu.roll(c, 1, 0))
                lap += jnp.where(row_i == cy - 1, yh[p, 1, f, pl.ds(x, 1), :], pltpu.roll(c, cy - 1, 0))
                lap += jnp.where(lane_i == 0, 0.0, pltpu.roll(c, 1, 1))
                lap += jnp.where(lane_i == LANES - 1, 0.0, pltpu.roll(c, LANES - 1, 1))
                push = jnp.where(lane_i == LANES - 1, pltpu.roll(top, LANES - 1 - f, 1), 0.0)
                V[f, x] = V[f, x] + scale * lap + push
            return 0

        lax.fori_loop(0, cx, lap_row, 0)

        for k in range(1, n_gy):
            src = lax.rem(b + k, n_gy)
            wait_from(rx.at[p, src], m_recv.at[p, src])
        got = [rx[p, src] for src in range(n_gy)]
        replies = [jnp.zeros((8, LANES), F32) for _ in range(n_gy)]
        springs = []
        for j in range(n_blocks):
            rec = jnp.zeros((8, LANES), F32)
            for src in range(n_gy):
                moved = pltpu.roll(got[src], ((src - j) * group) % LANES, 1) if src != j else got[src]
                rec = jnp.where(lane // group == src, moved, rec)
            idx = nbr[j]
            state = part[j]
            diff = [take_lanes(rows8(state[f:f + 1]), idx) - rec[f:f + 1] for f in range(6)]
            gain = rec[6:7] / (1.0 + diff[0] * diff[0] + diff[1] * diff[1] + diff[2] * diff[2])
            force = jnp.zeros((8, LANES), F32)
            for f in range(3):
                spring = gain * (PARTICLE_K * diff[f])
                springs.append(spring)
                total = jnp.sum(spring + gain * (DRAG_COEF * diff[3 + f]), axis=0, keepdims=True)
                force = jnp.where(sub == f, total, force)
            force = force * (1.0 / n_nbr)
            for src in range(n_gy):
                moved = pltpu.roll(force, ((j - src) * group) % LANES, 1) if src != j else force
                replies[src] = jnp.where(lane // group == j, moved, replies[src])
        for src in range(n_gy):
            ans[src] = replies[src]
        ax[p, b] = ans[b]
        a_copies = []
        for k in range(1, n_gy):
            o = lax.rem(b + k, n_gy)
            a_copies.append(remote(ans.at[o], ax.at[p, b], a_send.at[k], a_recv.at[p, b], (a, o)))
            a_copies[-1].start()

        for j in range(n_blocks):
            parts = [two_parts(springs[3 * j + f]) for f in range(3)]
            lhs = jnp.concatenate([q[0] for q in parts] + [q[1] for q in parts], axis=0).astype(BF16)
            wide = dot_nt(lhs, nbr_hot[j])
            change = jnp.zeros((8, LANES), F32)
            for f in range(3):
                acc = jnp.zeros((8, LANES), F32)
                for k in range(n_nbr):
                    ks = slice(k * LANES, (k + 1) * LANES)
                    acc = jnp.where(sub == k, wide[8 * f:8 * f + 8, ks] + wide[24 + 8 * f:32 + 8 * f, ks], acc)
                total = jnp.sum(acc, axis=0, keepdims=True) * (-TIME_STEP / n_nbr)
                change = change + jnp.where(sub == 3 + f, total, 0.0)
            state = part[j] + change
            part[j] = state + jnp.where(sub < 3, TIME_STEP * pltpu.roll(state, 5, 0), 0.0)

        for k in range(1, n_gy):
            src = lax.rem(b + k, n_gy)
            wait_from(ax.at[p, src], a_recv.at[p, src])
        cell_row = cells_v[pl.ds(s, 1), :]
        own_row = owner_v[pl.ds(s, 1), :]
        rank_row = rank[pl.ds(s, 1), :]
        zrow = lax.broadcasted_iota(jnp.int32, (LANES, LANES), 0)
        for w in range(rec_tiles):
            ws = slice(w * LANES, (w + 1) * LANES)
            own8, rank8 = rows8(own_row[:, ws]), rows8(rank_row[:, ws])
            force = jnp.zeros((8, LANES), F32)
            for o in range(n_gy):
                force = jnp.where(own8 == o, take_lanes(ax[p, o], rank8), force)
            push = TIME_STEP * force / recs[w][6:7]
            hi, lo = two_parts(push)
            here = zrow == (cell_row[:, ws] & 127)
            for f in range(3):
                b_hi[f * LANES:(f + 1) * LANES, ws] = jnp.where(here, hi[f:f + 1], 0.0).astype(BF16)
                b_lo[f * LANES:(f + 1) * LANES, ws] = jnp.where(here, lo[f:f + 1], 0.0).astype(BF16)
        for copy in m_copies + a_copies + [p_copy]:
            copy.wait_send()
        for there, copy, _k in halos + y_halos:
            @pl.when(there)
            def _(copy=copy):
                copy.wait_send()

        col_row = cell_row >> 7

        def add_chunk(i, _):
            x0 = i * chunk_x
            cols = lax.broadcasted_iota(jnp.int32, (chunk, n_rec), 0) + i * chunk
            hot = jnp.where(cols == col_row, 1.0, 0.0).astype(BF16)
            base = pl.multiple_of(i * (chunk * 8), chunk * 8)
            for f in range(3):
                fs = pl.ds(f * LANES, LANES)
                add = dot_nt(hot, b_hi[fs, :]) + dot_nt(hot, b_lo[fs, :])
                v = V[f, pl.ds(x0, chunk_x)].reshape(chunk, LANES) + add
                d = D[f, pl.ds(x0 + 1, chunk_x)].reshape(chunk, LANES) + TIME_STEP * v
                V[f, pl.ds(x0, chunk_x)] = v.reshape(chunk_x, cy, LANES)
                D[f, pl.ds(x0 + 1, chunk_x)] = d.reshape(chunk_x, cy, LANES)
                flat[pl.ds(base + f, chunk, stride=8), :] = d
                flat[pl.ds(base + 3 + f, chunk, stride=8), :] = v
                for xx in range(chunk_x):
                    ye[0, f, pl.ds(x0 + xx, 1), :] = d[xx * cy:xx * cy + 1]
                    ye[1, f, pl.ds(x0 + xx, 1), :] = d[xx * cy + cy - 1:xx * cy + cy]
            return 0

        lax.fori_loop(0, cx // chunk_x, add_chunk, 0)
        return 0

    lax.fori_loop(0, steps, step, 0)
    out_d = pltpu.make_async_copy(D.at[:, pl.ds(1, cx)], disp_out, out_sem.at[0])
    out_v = pltpu.make_async_copy(V, vel_out, out_sem.at[1])
    out_d.start()
    out_v.start()
    out_d.wait()
    out_v.wait()


def local(n_gx, n_gy, disp, vel, stiff, mass, contact_cells, contact_match, eroded, owners, bpos, bvel, bnbr):
    cx, cy, nz = disp.shape[1:]
    steps, n_rec = eroded.shape[0], eroded.shape[3]
    n_seg = contact_cells.shape[2]
    n_slots = bpos.shape[3]
    n_blocks = n_slots // LANES
    n_nbr = bnbr.shape[2]
    dims = (n_gx, n_gy, cx, cy, steps, n_rec, n_seg, n_blocks, n_nbr)
    contact = contact_cells.reshape(1, n_seg)
    cells = eroded.reshape(steps, n_rec)
    vm = pl.BlockSpec(memory_space=pltpu.VMEM)
    sm = pl.BlockSpec(memory_space=pltpu.SMEM)
    dma = pltpu.SemaphoreType.DMA
    tile = (8, LANES)
    return pl.pallas_call(
        functools.partial(kernel, dims),
        out_shape=(jax.ShapeDtypeStruct(disp.shape, F32), jax.ShapeDtypeStruct(vel.shape, F32)),
        in_specs=[sm, sm] + [vm] * 11,
        out_specs=(pl.BlockSpec(memory_space=pl.ANY), pl.BlockSpec(memory_space=pl.ANY)),
        scratch_shapes=[
            pltpu.VMEM((3, cx + 2, cy, nz), F32),
            pltpu.VMEM((3, cx, cy, nz), F32),
            pltpu.VMEM((cx, cy, nz), F32),
            pltpu.VMEM((cx * cy, 8, nz), F32),
            pltpu.VMEM((cx * cy, nz), F32),
            pltpu.VMEM((2, 3, cx, nz), F32),
            pltpu.VMEM((2, 2, 3, cx, nz), F32),
            pltpu.VMEM((2, 2, 3, cy, nz), F32),
            pltpu.VMEM((n_gy,) + tile, F32),
            pltpu.VMEM((2, n_gy) + tile, F32),
            pltpu.VMEM((n_gy,) + tile, F32),
            pltpu.VMEM((2, n_gy) + tile, F32),
            pltpu.VMEM((n_seg // LANES,) + tile, F32),
            pltpu.VMEM((2, n_seg // LANES) + tile, F32),
            pltpu.VMEM((steps, n_gy, LANES), jnp.int32),
            pltpu.VMEM((steps, n_rec), jnp.int32),
            pltpu.VMEM((n_blocks,) + tile, F32),
            pltpu.VMEM((n_blocks,) + tile, jnp.int32),
            pltpu.VMEM((n_blocks, n_nbr * LANES, LANES), BF16),
            pltpu.VMEM((cx * cy, n_seg), BF16),
            pltpu.VMEM((3 * LANES, n_rec), BF16),
            pltpu.VMEM((3 * LANES, n_rec), BF16),
            dma((2,)),
            dma((2,)), dma((2, 2)),
            dma((2,)), dma((2, 2)),
            dma((n_gy,)), dma((2, n_gy)),
            dma((n_gy,)), dma((2, n_gy)),
            dma, dma((2,)),
        ],
        compiler_params=pltpu.CompilerParams(collective_id=0, has_side_effects=True, vmem_limit_bytes=48 * 2**20),
        name="dynamics",
    )(
        cells, contact, disp, vel, stiff, mass, contact, contact_match.reshape(1, n_seg), cells,
        owners.reshape(steps, n_rec), bpos[0, 0], bvel[0, 0], bnbr[0, 0],
    )


def solution(mesh):
    return jax.shard_map(
        functools.partial(local, mesh.shape["gx"], mesh.shape["gy"]),
        mesh=mesh,
        in_specs=(
            P(None, "gx", "gy", None),
            P(None, "gx", "gy", None),
            P("gx", "gy", None),
            P("gx", "gy", None),
            P("gx", "gy", None),
            P("gx", "gy", None),
            P(None, "gx", "gy", None),
            P(None, "gx", "gy", None, None),
            P("gx", "gy", None, None),
            P("gx", "gy", None, None),
            P("gx", "gy", None, None),
        ),
        out_specs=(P(None, "gx", "gy", None), P(None, "gx", "gy", None)),
        check_vma=False,
    )
```

```python
import functools

import jax
import jax.numpy as jnp
from jax import lax
from jax.experimental import pallas as pl
from jax.experimental.pallas import tpu as pltpu
from jax.sharding import PartitionSpec as P

TIME_STEP = 0.2
CONTACT_K = 0.5
PARTICLE_K = 1.0
DRAG_COEF = 0.5
LANES = 128
F32 = jnp.float32
BF16 = jnp.bfloat16
MESH = pl.DeviceIdType.MESH


def take_lanes(x, idx):
    return jnp.take_along_axis(x, idx, axis=1, mode="promise_in_bounds")


def dot_nt(a, b):
    return lax.dot_general(a, b, (((1,), (1,)), ((), ())), preferred_element_type=F32)


def two_parts(x):
    hi = x.astype(BF16).astype(F32)
    return hi, x - hi


def rows8(row):
    return jnp.broadcast_to(row, (8, row.shape[1]))


def kernel(
    dims,
    cells_s, contact_s, disp_in, vel_in, stiff_in, mass_in, contact_v, match_v, cells_v, owner_v, bpos, bvel, bnbr,
    disp_out, vel_out,
    D, V, A, M, G, recs_buf, near, rec_hot, top_add, ye, yh, xh, msg, rx, ans, ax, seg, ps, inv, rank, part, nbr, nbr_hot, seg_hot, b_both,
    out_sem, in_sem, ye_send, yh_recv, xe_send, xh_recv, m_send, m_recv, a_send, a_recv, p_send, p_recv,
):
    n_gx, n_gy, cx, cy, steps, n_rec, n_seg, n_blocks, n_nbr = dims
    n_cols = cx * cy
    group = LANES // n_gy
    rec_tiles = n_rec // LANES
    seg_tiles = n_seg // LANES
    chunk_x = 8
    chunk = chunk_x * cy
    a = lax.axis_index("gx")
    b = lax.axis_index("gy")
    mate = a + 1 - 2 * lax.rem(a, 2)
    lane = lax.broadcasted_iota(jnp.int32, (8, LANES), 1)
    sub = lax.broadcasted_iota(jnp.int32, (8, LANES), 0)

    flat = G.reshape(n_cols * 8, LANES)

    loads = [
        pltpu.make_async_copy(disp_in, D.at[:, pl.ds(1, cx)], in_sem.at[0]),
        pltpu.make_async_copy(vel_in, V, in_sem.at[1]),
        pltpu.make_async_copy(stiff_in, A, in_sem.at[2]),
        pltpu.make_async_copy(mass_in, M, in_sem.at[3]),
    ]
    for load in loads:
        load.start()
    yh[...] = jnp.zeros_like(yh)
    xh[...] = jnp.zeros_like(xh)


    tri = jnp.where(
        lax.broadcasted_iota(jnp.int32, (n_rec, n_rec), 1) <= lax.broadcasted_iota(jnp.int32, (n_rec, n_rec), 0), 1.0, 0.0
    ).astype(BF16)

    def init_step(s, _):
        own = owner_v[s, 0]
        mine = lax.broadcasted_iota(jnp.int32, (n_gy, n_rec), 0) == own
        hot = jnp.where(mine, 1.0, 0.0)
        counted = dot_nt(jnp.concatenate([hot] * 2, axis=0).astype(BF16), tri)[:n_gy]
        rk = (jnp.sum(hot * counted, axis=0, keepdims=True) - 1.0).astype(jnp.int32)
        rank[pl.ds(s, 1), :] = rk
        rec = lax.broadcasted_iota(jnp.int32, (n_gy, n_rec), 1) + 1
        lo = jnp.where(mine, (rec & 127).astype(F32), 0.0)
        hi = jnp.where(mine, (rec >> 7).astype(F32), 0.0)
        q_hot = jnp.where(lax.broadcasted_iota(jnp.int32, (LANES, n_rec), 0) == rk, 1.0, 0.0).astype(BF16)
        both = dot_nt(jnp.concatenate([lo, hi], axis=0).astype(BF16), q_hot)
        inv[s] = (both[:n_gy] + 128.0 * both[n_gy:]).astype(jnp.int32) - 1
        return 0

    lax.fori_loop(0, steps, init_step, 0)

    perm = lax.rem(lane, group) * n_gy + lane // group
    nrow = lax.broadcasted_iota(jnp.int32, (LANES, LANES), 0)

    def init_block(j, _):
        at = pl.ds(pl.multiple_of(j * LANES, LANES), LANES)
        rows = jnp.concatenate([bpos[:, at], bvel[:, at], jnp.zeros((2, LANES), F32)], axis=0)
        part[j] = take_lanes(rows, perm)
        old = take_lanes(bnbr[:, at], perm)
        new = lax.rem(old, n_gy) * group + old // n_gy
        nbr[j] = new
        for k in range(n_nbr):
            nbr_hot[j, pl.ds(k * LANES, LANES), :] = jnp.where(nrow == new[k:k + 1], 1.0, 0.0).astype(BF16)
        return 0

    lax.fori_loop(0, n_blocks, init_block, 0)

    for load in loads:
        load.wait()

    def init_chunk(i, _):
        x0 = i * chunk_x
        xs = pl.ds(x0, chunk_x)
        m = M[xs].reshape(chunk, LANES)
        A[xs] = TIME_STEP * A[xs] / M[xs]
        base = pl.multiple_of(i * (chunk * 8), chunk * 8)
        for f in range(3):
            d = D[f, pl.ds(x0 + 1, chunk_x)]
            v = V[f, xs]
            flat[pl.ds(base + f, chunk, stride=8), :] = d.reshape(chunk, LANES)
            flat[pl.ds(base + 3 + f, chunk, stride=8), :] = v.reshape(chunk, LANES)
            for xx in range(chunk_x):
                ye[0, f, pl.ds(x0 + xx, 1), :] = d[xx, 0:1]
                ye[1, f, pl.ds(x0 + xx, 1), :] = d[xx, cy - 1:cy]
        flat[pl.ds(base + 6, chunk, stride=8), :] = m
        flat[pl.ds(base + 7, chunk, stride=8), :] = jnp.zeros_like(m)
        cols = lax.broadcasted_iota(jnp.int32, (chunk, n_seg), 0) + i * chunk
        seg_hot[pl.ds(pl.multiple_of(i * chunk, chunk), chunk), :] = jnp.where(cols == contact_v[...], 1.0, 0.0).astype(BF16)
        return 0

    lax.fori_loop(0, cx // chunk_x, init_chunk, 0)

    barrier = pltpu.get_barrier_semaphore()
    for k in range(1, n_gy):
        pl.semaphore_signal(barrier, inc=1, device_id=(a, lax.rem(b + k, n_gy)), device_id_type=MESH)

    @pl.when(a > 0)
    def _():
        pl.semaphore_signal(barrier, inc=1, device_id=(a - 1, b), device_id_type=MESH)

    @pl.when(a < n_gx - 1)
    def _():
        pl.semaphore_signal(barrier, inc=1, device_id=(a + 1, b), device_id_type=MESH)

    n_near = jnp.where(a > 0, 1, 0) + jnp.where(a < n_gx - 1, 1, 0)
    pl.semaphore_wait(barrier, n_gy - 1 + n_near)

    def remote(src, dst, send, recv, to):
        return pltpu.make_async_remote_copy(src_ref=src, dst_ref=dst, send_sem=send, recv_sem=recv, device_id=to, device_id_type=MESH)

    def step(s, _):
        p = lax.rem(s, 2)
        halos = (
            (a > 0, remote(D.at[:, 1], xh.at[p, 1], xe_send.at[0], xh_recv.at[p, 1], (a - 1, b)), 0),
            (a < n_gx - 1, remote(D.at[:, cx], xh.at[p, 0], xe_send.at[1], xh_recv.at[p, 0], (a + 1, b)), 1),
        )
        y_halos = (
            (b > 0, remote(ye.at[0], yh.at[p, 1], ye_send.at[0], yh_recv.at[p, 1], (a, b - 1)), 0),
            (b < n_gy - 1, remote(ye.at[1], yh.at[p, 0], ye_send.at[1], yh_recv.at[p, 0], (a, b + 1)), 1),
        )

        for there, copy, _k in halos + y_halos:
            @pl.when(there)
            def _(copy=copy):
                copy.start()

        def read_rec(w, _):
            acc = jnp.zeros((8, LANES), F32)
            for t in range(LANES):
                cell = cells_s[s, 0, 0, w * LANES + t]
                acc = jnp.where(lane == t, take_lanes(G[cell >> 7], jnp.full((8, LANES), cell & 127, jnp.int32)), acc)
            recs_buf[w] = acc
            return 0

        lax.fori_loop(0, rec_tiles, read_rec, 0)
        recs = [recs_buf[w] for w in range(rec_tiles)]
        for o in range(n_gy):
            idx = rows8(inv[s, o:o + 1, :])
            out = jnp.zeros((8, LANES), F32)
            for w in range(rec_tiles):
                out = jnp.where((idx >> 7) == w, take_lanes(recs[w], idx & 127), out)
            msg[o] = out
        rx[p, b] = msg[b]
        m_copies = []
        for k in range(1, n_gy):
            o = lax.rem(b + k, n_gy)
            m_copies.append(remote(msg.at[o], rx.at[p, b], m_send.at[k], m_recv.at[p, b], (a, o)))
            m_copies[-1].start()
        def read_seg(w, _):
            acc = jnp.zeros((8, LANES), F32)
            for t in range(LANES):
                acc = jnp.where(lane == t, pltpu.roll(G[contact_s[0, w * LANES + t]], (t + 1) % LANES, 1), acc)
            seg[w] = acc
            return 0

        lax.fori_loop(0, seg_tiles, read_seg, 0)
        p_copy = remote(seg, ps.at[p], p_send, p_recv.at[p], (mate, b))
        p_copy.start()

        def wait_from(dst, recv):
            pltpu.make_async_copy(dst, dst, recv).wait()

        @pl.when(a > 0)
        def _():
            wait_from(xh.at[p, 0], xh_recv.at[p, 0])

        @pl.when(a < n_gx - 1)
        def _():
            wait_from(xh.at[p, 1], xh_recv.at[p, 1])

        @pl.when(b > 0)
        def _():
            wait_from(yh.at[p, 0], yh_recv.at[p, 0])

        @pl.when(b < n_gy - 1)
        def _():
            wait_from(yh.at[p, 1], yh_recv.at[p, 1])

        D[:, 0] = xh[p, 0]
        D[:, cx + 1] = xh[p, 1]
        wait_from(ps.at[p], p_recv.at[p])
        c_parts = [[], []]
        for w in range(seg_tiles):
            idx = rows8(match_v[:, w * LANES:(w + 1) * LANES])
            facing = jnp.zeros((8, LANES), F32)
            for u in range(seg_tiles):
                facing = jnp.where((idx >> 7) == u, take_lanes(ps[p, u], idx & 127), facing)
            own = seg[w]
            pull = (TIME_STEP * CONTACT_K) * (facing - own) / own[6:7]
            hi, lo = two_parts(pltpu.roll(jnp.where(sub < 3, pull, 0.0), 5, 0))
            c_parts[0].append(hi)
            c_parts[1].append(lo)
        zero_rows = jnp.zeros((LANES - 8, n_seg), F32)
        c_mats = [jnp.concatenate([zero_rows, jnp.concatenate(part_, axis=1)], axis=0).astype(BF16) for part_ in c_parts]

        def top_chunk(i, _):
            at = pl.ds(pl.multiple_of(i * chunk, chunk), chunk)
            hot = seg_hot[at, :]
            top_add[at, :] = dot_nt(hot, c_mats[0]) + dot_nt(hot, c_mats[1])
            return 0

        lax.fori_loop(0, cx // chunk_x, top_chunk, 0)

        row_i = lax.broadcasted_iota(jnp.int32, (cy, LANES), 0)
        lane_i = lax.broadcasted_iota(jnp.int32, (cy, LANES), 1)

        def lap_row(x):
            top = top_add[pl.ds(pl.multiple_of(x * cy, cy), cy), :]
            scale = A[x]
            for f in range(3):
                c = D[f, x + 1]
                lap = D[f, x] + D[f, x + 2] - 6.0 * c
                lap += jnp.where(row_i == 0, yh[p, 0, f, pl.ds(x, 1), :], pltpu.roll(c, 1, 0))
                lap += jnp.where(row_i == cy - 1, yh[p, 1, f, pl.ds(x, 1), :], pltpu.roll(c, cy - 1, 0))
                lap += jnp.where(lane_i == 0, 0.0, pltpu.roll(c, 1, 1))
                lap += jnp.where(lane_i == LANES - 1, 0.0, pltpu.roll(c, LANES - 1, 1))
                push = jnp.where(lane_i == LANES - 1, pltpu.roll(top, 2 - f, 1) if f < 2 else top, 0.0)
                V[f, x] = V[f, x] + scale * lap + push

        def lap_rows(i, _):
            lap_row(2 * i)
            lap_row(2 * i + 1)
            return 0

        lax.fori_loop(0, cx // 4, lap_rows, 0)
        for j in range(n_blocks):
            state = part[j]
            idx = nbr[j]
            for f in range(6):
                near[j, f] = take_lanes(rows8(state[f:f + 1]), idx)

        for k in range(1, n_gy):
            src = lax.rem(b + k, n_gy)
            wait_from(rx.at[p, src], m_recv.at[p, src])
        got = [rx[p, src] for src in range(n_gy)]
        replies = [jnp.zeros((8, LANES), F32) for _ in range(n_gy)]
        springs = []
        for j in range(n_blocks):
            rec = jnp.zeros((8, LANES), F32)
            for src in range(n_gy):
                moved = pltpu.roll(got[src], ((src - j) * group) % LANES, 1) if src != j else got[src]
                rec = jnp.where(lane // group == src, moved, rec)
            diff = [near[j, f] - rec[f:f + 1] for f in range(6)]
            gain = rec[6:7] / (1.0 + diff[0] * diff[0] + diff[1] * diff[1] + diff[2] * diff[2])
            force = jnp.zeros((8, LANES), F32)
            for f in range(3):
                spring = gain * (PARTICLE_K * diff[f])
                springs.append(spring)
                total = jnp.sum(spring + gain * (DRAG_COEF * diff[3 + f]), axis=0, keepdims=True)
                force = jnp.where(sub == f, total, force)
            force = force * (1.0 / n_nbr)
            for src in range(n_gy):
                moved = pltpu.roll(force, ((j - src) * group) % LANES, 1) if src != j else force
                replies[src] = jnp.where(lane // group == j, moved, replies[src])
        for src in range(n_gy):
            ans[src] = replies[src]
        ax[p, b] = ans[b]
        a_copies = []
        for k in range(1, n_gy):
            o = lax.rem(b + k, n_gy)
            a_copies.append(remote(ans.at[o], ax.at[p, b], a_send.at[k], a_recv.at[p, b], (a, o)))
            a_copies[-1].start()

        for j in range(n_blocks):
            parts = [two_parts(springs[3 * j + f]) for f in range(3)]
            lhs = jnp.concatenate([q[0] for q in parts] + [q[1] for q in parts], axis=0).astype(BF16)
            wide = dot_nt(lhs, nbr_hot[j])
            change = jnp.zeros((8, LANES), F32)
            for f in range(3):
                acc = jnp.zeros((8, LANES), F32)
                for k in range(n_nbr):
                    ks = slice(k * LANES, (k + 1) * LANES)
                    acc = jnp.where(sub == k, wide[8 * f:8 * f + 8, ks] + wide[24 + 8 * f:32 + 8 * f, ks], acc)
                total = jnp.sum(acc, axis=0, keepdims=True) * (-TIME_STEP / n_nbr)
                change = change + jnp.where(sub == 3 + f, total, 0.0)
            state = part[j] + change
            part[j] = state + jnp.where(sub < 3, TIME_STEP * pltpu.roll(state, 5, 0), 0.0)

        lax.fori_loop(cx // 4, cx // 2, lap_rows, 0)
        cell_row = cells_v[s, 0]
        col_row = cell_row >> 7

        def hot_chunk(i, _):
            cols = lax.broadcasted_iota(jnp.int32, (chunk, n_rec), 0) + i * chunk
            rec_hot[pl.ds(pl.multiple_of(i * chunk, chunk), chunk), :] = jnp.where(cols == col_row, 1.0, 0.0).astype(BF16)
            return 0

        lax.fori_loop(0, cx // chunk_x, hot_chunk, 0)

        for k in range(1, n_gy):
            src = lax.rem(b + k, n_gy)
            wait_from(ax.at[p, src], a_recv.at[p, src])
        own_row = owner_v[s, 0]
        rank_row = rank[pl.ds(s, 1), :]
        zrow = lax.broadcasted_iota(jnp.int32, (LANES, LANES), 0)
        for w in range(rec_tiles):
            ws = slice(w * LANES, (w + 1) * LANES)
            own8, rank8 = rows8(own_row[:, ws]), rows8(rank_row[:, ws])
            force = jnp.zeros((8, LANES), F32)
            for o in range(n_gy):
                force = jnp.where(own8 == o, take_lanes(ax[p, o], rank8), force)
            push = TIME_STEP * force / recs[w][6:7]
            hi, lo = two_parts(push)
            here = zrow == (cell_row[:, ws] & 127)
            for f in range(3):
                b_both[2 * f * LANES:(2 * f + 1) * LANES, ws] = jnp.where(here, hi[f:f + 1], 0.0).astype(BF16)
                b_both[(2 * f + 1) * LANES:(2 * f + 2) * LANES, ws] = jnp.where(here, lo[f:f + 1], 0.0).astype(BF16)
        for copy in m_copies + a_copies + [p_copy]:
            copy.wait_send()
        for there, copy, _k in halos + y_halos:
            @pl.when(there)
            def _(copy=copy):
                copy.wait_send()

        def add_chunk(i, _):
            x0 = i * chunk_x
            hot = rec_hot[pl.ds(pl.multiple_of(i * chunk, chunk), chunk), :]
            base = pl.multiple_of(i * (chunk * 8), chunk * 8)
            for f in range(3):
                both = dot_nt(hot, b_both[pl.ds(2 * f * LANES, 2 * LANES), :])
                add = both[:, :LANES] + both[:, LANES:]
                v = V[f, pl.ds(x0, chunk_x)].reshape(chunk, LANES) + add
                d = D[f, pl.ds(x0 + 1, chunk_x)].reshape(chunk, LANES) + TIME_STEP * v
                V[f, pl.ds(x0, chunk_x)] = v.reshape(chunk_x, cy, LANES)
                D[f, pl.ds(x0 + 1, chunk_x)] = d.reshape(chunk_x, cy, LANES)
                flat[pl.ds(base + f, chunk, stride=8), :] = d
                flat[pl.ds(base + 3 + f, chunk, stride=8), :] = v
                for xx in range(chunk_x):
                    ye[0, f, pl.ds(x0 + xx, 1), :] = d[xx * cy:xx * cy + 1]
                    ye[1, f, pl.ds(x0 + xx, 1), :] = d[xx * cy + cy - 1:xx * cy + cy]
            return 0

        lax.fori_loop(0, cx // chunk_x, add_chunk, 0)
        return 0

    lax.fori_loop(0, steps, step, 0)
    out_d = pltpu.make_async_copy(D.at[:, pl.ds(1, cx)], disp_out, out_sem.at[0])
    out_v = pltpu.make_async_copy(V, vel_out, out_sem.at[1])
    out_d.start()
    out_v.start()
    out_d.wait()
    out_v.wait()


def local(n_gx, n_gy, disp, vel, stiff, mass, contact_cells, contact_match, eroded, owners, bpos, bvel, bnbr):
    cx, cy, nz = disp.shape[1:]
    steps, n_rec = eroded.shape[0], eroded.shape[3]
    n_seg = contact_cells.shape[2]
    n_slots = bpos.shape[3]
    n_blocks = n_slots // LANES
    n_nbr = bnbr.shape[2]
    dims = (n_gx, n_gy, cx, cy, steps, n_rec, n_seg, n_blocks, n_nbr)
    contact = contact_cells.reshape(1, n_seg)
    cells = eroded.reshape(steps, 1, 1, n_rec)
    vm = pl.BlockSpec(memory_space=pltpu.VMEM)
    sm = pl.BlockSpec(memory_space=pltpu.SMEM)
    anywhere = pl.BlockSpec(memory_space=pl.ANY)
    dma = pltpu.SemaphoreType.DMA
    tile = (8, LANES)
    return pl.pallas_call(
        functools.partial(kernel, dims),
        out_shape=(jax.ShapeDtypeStruct(disp.shape, F32), jax.ShapeDtypeStruct(vel.shape, F32)),
        in_specs=[sm, sm] + [anywhere] * 4 + [vm] * 7,
        out_specs=(anywhere, anywhere),
        scratch_shapes=[
            pltpu.VMEM((3, cx + 2, cy, nz), F32),
            pltpu.VMEM((3, cx, cy, nz), F32),
            pltpu.VMEM((cx, cy, nz), F32),
            pltpu.VMEM((cx, cy, nz), F32),
            pltpu.VMEM((cx * cy, 8, nz), F32),
            pltpu.VMEM((n_rec // LANES,) + tile, F32),
            pltpu.VMEM((n_blocks, 6) + tile, F32),
            pltpu.VMEM((cx * cy, n_rec), BF16),
            pltpu.VMEM((cx * cy, nz), F32),
            pltpu.VMEM((2, 3, cx, nz), F32),
            pltpu.VMEM((2, 2, 3, cx, nz), F32),
            pltpu.VMEM((2, 2, 3, cy, nz), F32),
            pltpu.VMEM((n_gy,) + tile, F32),
            pltpu.VMEM((2, n_gy) + tile, F32),
            pltpu.VMEM((n_gy,) + tile, F32),
            pltpu.VMEM((2, n_gy) + tile, F32),
            pltpu.VMEM((n_seg // LANES,) + tile, F32),
            pltpu.VMEM((2, n_seg // LANES) + tile, F32),
            pltpu.VMEM((steps, n_gy, LANES), jnp.int32),
            pltpu.VMEM((steps, n_rec), jnp.int32),
            pltpu.VMEM((n_blocks,) + tile, F32),
            pltpu.VMEM((n_blocks,) + tile, jnp.int32),
            pltpu.VMEM((n_blocks, n_nbr * LANES, LANES), BF16),
            pltpu.VMEM((cx * cy, n_seg), BF16),
            pltpu.VMEM((6 * LANES, n_rec), BF16),
            dma((2,)), dma((4,)),
            dma((2,)), dma((2, 2)),
            dma((2,)), dma((2, 2)),
            dma((n_gy,)), dma((2, n_gy)),
            dma((n_gy,)), dma((2, n_gy)),
            dma, dma((2,)),
        ],
        compiler_params=pltpu.CompilerParams(collective_id=0, has_side_effects=True, vmem_limit_bytes=60 * 2**20),
        name="dynamics",
    )(
        cells, contact, disp, vel, stiff, mass, contact, contact_match.reshape(1, n_seg), cells,
        owners.reshape(steps, 1, 1, n_rec), bpos[0, 0], bvel[0, 0], bnbr[0, 0],
    )


def solution(mesh):
    return jax.shard_map(
        functools.partial(local, mesh.shape["gx"], mesh.shape["gy"]),
        mesh=mesh,
        in_specs=(
            P(None, "gx", "gy", None),
            P(None, "gx", "gy", None),
            P("gx", "gy", None),
            P("gx", "gy", None),
            P("gx", "gy", None),
            P("gx", "gy", None),
            P(None, "gx", "gy", None),
            P(None, "gx", "gy", None, None),
            P("gx", "gy", None, None),
            P("gx", "gy", None, None),
            P("gx", "gy", None, None),
        ),
        out_specs=(P(None, "gx", "gy", None), P(None, "gx", "gy", None)),
        check_vma=False,
    )
```

```python
import functools

import jax
import jax.numpy as jnp
from jax import lax
from jax.experimental import pallas as pl
from jax.experimental.pallas import tpu as pltpu
from jax.sharding import PartitionSpec as P

TIME_STEP = 0.2
CONTACT_K = 0.5
PARTICLE_K = 1.0
DRAG_COEF = 0.5
LANES = 128
F32 = jnp.float32
BF16 = jnp.bfloat16
MESH = pl.DeviceIdType.MESH


def take_lanes(x, idx):
    return jnp.take_along_axis(x, idx, axis=1, mode="promise_in_bounds")


def dot_nt(a, b):
    return lax.dot_general(a, b, (((1,), (1,)), ((), ())), preferred_element_type=F32)


def two_parts(x):
    hi = x.astype(BF16).astype(F32)
    return hi, x - hi


def rows8(row):
    return jnp.broadcast_to(row, (8, row.shape[1]))


def kernel(
    dims,
    cells_s, contact_s, disp_in, vel_in, stiff_in, mass_in, contact_v, match_v, cells_v, owner_v, bpos, bvel, bnbr,
    disp_out, vel_out,
    D, V, A, M, G, recs_buf, seg_pre, push_buf, near, match_hot, cell_col, top_add, ye, yh, xh, msg, rx, ans, ax, seg, ps, inv, rank, part, nbr, nbr_hot, seg_hot, b_both,
    out_sem, in_sem, ye_send, yh_recv, xe_send, xh_recv, m_send, m_recv, a_send, a_recv, p_send, p_recv,
):
    n_gx, n_gy, cx, cy, steps, n_rec, n_seg, n_blocks, n_nbr = dims
    n_cols = cx * cy
    group = LANES // n_gy
    rec_tiles = n_rec // LANES
    seg_tiles = n_seg // LANES
    chunk_x = 8
    chunk = chunk_x * cy
    a = lax.axis_index("gx")
    b = lax.axis_index("gy")
    mate = a + 1 - 2 * lax.rem(a, 2)
    lane = lax.broadcasted_iota(jnp.int32, (8, LANES), 1)
    sub = lax.broadcasted_iota(jnp.int32, (8, LANES), 0)

    flat = G.reshape(n_cols * 8, LANES)

    loads = [
        pltpu.make_async_copy(disp_in, D.at[:, pl.ds(1, cx)], in_sem.at[0]),
        pltpu.make_async_copy(vel_in, V, in_sem.at[1]),
        pltpu.make_async_copy(stiff_in, A, in_sem.at[2]),
        pltpu.make_async_copy(mass_in, M, in_sem.at[3]),
    ]
    for load in loads:
        load.start()
    yh[...] = jnp.zeros_like(yh)
    xh[...] = jnp.zeros_like(xh)
    push_buf[...] = jnp.zeros_like(push_buf)


    tri = jnp.where(
        lax.broadcasted_iota(jnp.int32, (n_rec, n_rec), 1) <= lax.broadcasted_iota(jnp.int32, (n_rec, n_rec), 0), 1.0, 0.0
    ).astype(BF16)

    def init_step(s, _):
        own = owner_v[s, 0]
        mine = lax.broadcasted_iota(jnp.int32, (n_gy, n_rec), 0) == own
        hot = jnp.where(mine, 1.0, 0.0)
        counted = dot_nt(jnp.concatenate([hot] * 2, axis=0).astype(BF16), tri)[:n_gy]
        rk = (jnp.sum(hot * counted, axis=0, keepdims=True) - 1.0).astype(jnp.int32)
        rank[pl.ds(s, 1), :] = rk
        rec = lax.broadcasted_iota(jnp.int32, (n_gy, n_rec), 1) + 1
        lo = jnp.where(mine, (rec & 127).astype(F32), 0.0)
        hi = jnp.where(mine, (rec >> 7).astype(F32), 0.0)
        q_hot = jnp.where(lax.broadcasted_iota(jnp.int32, (LANES, n_rec), 0) == rk, 1.0, 0.0).astype(BF16)
        both = dot_nt(jnp.concatenate([lo, hi], axis=0).astype(BF16), q_hot)
        inv[s] = (both[:n_gy] + 128.0 * both[n_gy:]).astype(jnp.int32) - 1
        cell_row = cells_v[s, 0].astype(F32)
        for w in range(rec_tiles):
            ws = slice(w * LANES, (w + 1) * LANES)
            cell_col[s, ws, :] = jnp.broadcast_to(cell_row[:, ws], (LANES, LANES)).T
        return 0

    lax.fori_loop(0, steps, init_step, 0)

    perm = lax.rem(lane, group) * n_gy + lane // group
    nrow = lax.broadcasted_iota(jnp.int32, (LANES, LANES), 0)

    def init_block(j, _):
        at = pl.ds(pl.multiple_of(j * LANES, LANES), LANES)
        rows = jnp.concatenate([bpos[:, at], bvel[:, at], jnp.zeros((2, LANES), F32)], axis=0)
        part[j] = take_lanes(rows, perm)
        old = take_lanes(bnbr[:, at], perm)
        new = lax.rem(old, n_gy) * group + old // n_gy
        nbr[j] = new
        for k in range(n_nbr):
            nbr_hot[j, pl.ds(k * LANES, LANES), :] = jnp.where(nrow == new[k:k + 1], 1.0, 0.0).astype(BF16)
        return 0

    lax.fori_loop(0, n_blocks, init_block, 0)

    for load in loads:
        load.wait()

    def init_chunk(i, _):
        x0 = i * chunk_x
        xs = pl.ds(x0, chunk_x)
        m = M[xs].reshape(chunk, LANES)
        A[xs] = TIME_STEP * A[xs] / M[xs]
        base = pl.multiple_of(i * (chunk * 8), chunk * 8)
        for f in range(3):
            d = D[f, pl.ds(x0 + 1, chunk_x)]
            v = V[f, xs]
            flat[pl.ds(base + f, chunk, stride=8), :] = d.reshape(chunk, LANES)
            flat[pl.ds(base + 3 + f, chunk, stride=8), :] = v.reshape(chunk, LANES)
            for xx in range(chunk_x):
                ye[0, f, pl.ds(x0 + xx, 1), :] = d[xx, 0:1]
                ye[1, f, pl.ds(x0 + xx, 1), :] = d[xx, cy - 1:cy]
        flat[pl.ds(base + 6, chunk, stride=8), :] = m
        flat[pl.ds(base + 7, chunk, stride=8), :] = jnp.zeros_like(m)
        cols = lax.broadcasted_iota(jnp.int32, (chunk, n_seg), 0) + i * chunk
        seg_hot[pl.ds(pl.multiple_of(i * chunk, chunk), chunk), :] = jnp.where(cols == contact_v[...], 1.0, 0.0).astype(BF16)
        return 0

    lax.fori_loop(0, cx // chunk_x, init_chunk, 0)

    barrier = pltpu.get_barrier_semaphore()
    for k in range(1, n_gy):
        pl.semaphore_signal(barrier, inc=1, device_id=(a, lax.rem(b + k, n_gy)), device_id_type=MESH)

    @pl.when(a > 0)
    def _():
        pl.semaphore_signal(barrier, inc=1, device_id=(a - 1, b), device_id_type=MESH)

    @pl.when(a < n_gx - 1)
    def _():
        pl.semaphore_signal(barrier, inc=1, device_id=(a + 1, b), device_id_type=MESH)

    n_near = jnp.where(a > 0, 1, 0) + jnp.where(a < n_gx - 1, 1, 0)
    pl.semaphore_wait(barrier, n_gy - 1 + n_near)

    def remote(src, dst, send, recv, to):
        return pltpu.make_async_remote_copy(src_ref=src, dst_ref=dst, send_sem=send, recv_sem=recv, device_id=to, device_id_type=MESH)

    def read_records(s):
        def read_rec(w, _):
            acc = jnp.zeros((8, LANES), F32)
            for t in range(LANES):
                cell = cells_s[s, 0, 0, w * LANES + t]
                acc = jnp.where(lane == t, take_lanes(G[cell >> 7], jnp.full((8, LANES), cell & 127, jnp.int32)), acc)
            recs_buf[w] = acc
            return 0

        lax.fori_loop(0, rec_tiles, read_rec, 0)

    def read_segments():
        def read_seg(w, _):
            acc = jnp.zeros((8, LANES), F32)
            for t in range(LANES):
                acc = jnp.where(lane == t, pltpu.roll(G[contact_s[0, w * LANES + t]], (t + 1) % LANES, 1), acc)
            seg_pre[w] = acc
            return 0

        lax.fori_loop(0, seg_tiles, read_seg, 0)

    def add_forces(s):
        cell_row = cells_v[s, 0]
        col_row = cell_row >> 7
        zrow = lax.broadcasted_iota(jnp.int32, (LANES, LANES), 0)
        for w in range(rec_tiles):
            ws = slice(w * LANES, (w + 1) * LANES)
            here = zrow == (cell_row[:, ws] & 127)
            for f in range(3):
                for q in range(2):
                    b_both[(2 * f + q) * LANES:(2 * f + q + 1) * LANES, ws] = jnp.where(
                        here, push_buf[q, w, f:f + 1, :], 0.0
                    ).astype(BF16)

        def add_chunk(i, _):
            x0 = i * chunk_x
            cols = lax.broadcasted_iota(jnp.int32, (chunk, n_rec), 0) + i * chunk
            hot = jnp.where(cols == col_row, 1.0, 0.0).astype(BF16)
            for f in range(3):
                both = dot_nt(hot, b_both[pl.ds(2 * f * LANES, 2 * LANES), :])
                add = both[:, :LANES] + both[:, LANES:]
                v = V[f, pl.ds(x0, chunk_x)].reshape(chunk, LANES) + add
                d = D[f, pl.ds(x0 + 1, chunk_x)].reshape(chunk, LANES) + TIME_STEP * v
                V[f, pl.ds(x0, chunk_x)] = v.reshape(chunk_x, cy, LANES)
                D[f, pl.ds(x0 + 1, chunk_x)] = d.reshape(chunk_x, cy, LANES)
                for xx in range(chunk_x):
                    ye[0, f, pl.ds(x0 + xx, 1), :] = d[xx * cy:xx * cy + 1]
                    ye[1, f, pl.ds(x0 + xx, 1), :] = d[xx * cy + cy - 1:xx * cy + cy]
            return 0

        lax.fori_loop(0, cx // chunk_x, add_chunk, 0)

    read_records(0)
    read_segments()
    for w in range(seg_tiles):
        seg[w] = seg_pre[w]

    def step(s, _):
        p = lax.rem(s, 2)
        after = jnp.minimum(s + 1, steps - 1)
        halos = (
            (a > 0, remote(D.at[:, 1], xh.at[p, 1], xe_send.at[0], xh_recv.at[p, 1], (a - 1, b)), 0),
            (a < n_gx - 1, remote(D.at[:, cx], xh.at[p, 0], xe_send.at[1], xh_recv.at[p, 0], (a + 1, b)), 1),
        )
        y_halos = (
            (b > 0, remote(ye.at[0], yh.at[p, 1], ye_send.at[0], yh_recv.at[p, 1], (a, b - 1)), 0),
            (b < n_gy - 1, remote(ye.at[1], yh.at[p, 0], ye_send.at[1], yh_recv.at[p, 0], (a, b + 1)), 1),
        )

        def wait_from(dst, recv):
            pltpu.make_async_copy(dst, dst, recv).wait()

        recs = [recs_buf[w] for w in range(rec_tiles)]
        for o in range(n_gy):
            idx = rows8(inv[s, o:o + 1, :])
            out = jnp.zeros((8, LANES), F32)
            for w in range(rec_tiles):
                out = jnp.where((idx >> 7) == w, take_lanes(recs[w], idx & 127), out)
            msg[o] = out
        rx[p, b] = msg[b]
        m_copies = []
        for k in range(1, n_gy):
            o = lax.rem(b + k, n_gy)
            m_copies.append(remote(msg.at[o], rx.at[p, b], m_send.at[k], m_recv.at[p, b], (a, o)))
            m_copies[-1].start()
        p_copy = remote(seg, ps.at[p], p_send, p_recv.at[p], (mate, b))
        p_copy.start()

        @pl.when(s > 0)
        def _():
            add_forces(s - 1)

        for there, copy, _k in halos + y_halos:
            @pl.when(there)
            def _(copy=copy):
                copy.start()

        goal = jnp.concatenate([cells_v[after, 0], contact_v[...] * LANES + (LANES - 1)], axis=1).astype(F32)

        def match_tile(w, _):
            at = pl.ds(pl.multiple_of(w * LANES, LANES), LANES)
            col = cell_col[s, at, :]
            for t in range(rec_tiles + seg_tiles):
                ts = slice(t * LANES, (t + 1) * LANES)
                match_hot[at, ts] = jnp.where(col == goal[:, ts], 1.0, 0.0).astype(BF16)
            return 0

        lax.fori_loop(0, rec_tiles, match_tile, 0)
        for j in range(n_blocks):
            state = part[j]
            idx = nbr[j]
            for f in range(6):
                near[j, f] = take_lanes(rows8(state[f:f + 1]), idx)

        wait_from(ps.at[p], p_recv.at[p])
        c_parts = [[], []]
        for w in range(seg_tiles):
            idx = rows8(match_v[:, w * LANES:(w + 1) * LANES])
            facing = jnp.zeros((8, LANES), F32)
            for u in range(seg_tiles):
                facing = jnp.where((idx >> 7) == u, take_lanes(ps[p, u], idx & 127), facing)
            own = seg[w]
            pull = (TIME_STEP * CONTACT_K) * (facing - own) / own[6:7]
            hi, lo = two_parts(pltpu.roll(jnp.where(sub < 3, pull, 0.0), 5, 0))
            c_parts[0].append(hi)
            c_parts[1].append(lo)
        zero_rows = jnp.zeros((LANES - 8, n_seg), F32)
        c_mat = jnp.concatenate(
            [zero_rows, jnp.concatenate(c_parts[0], axis=1), zero_rows, jnp.concatenate(c_parts[1], axis=1)], axis=0
        ).astype(BF16)

        def top_chunk(i, _):
            at = pl.ds(pl.multiple_of(i * chunk, chunk), chunk)
            hot = seg_hot[at, :]
            both = dot_nt(hot, c_mat)
            top_add[at, :] = both[:, :LANES] + both[:, LANES:]
            return 0

        lax.fori_loop(0, cx // chunk_x, top_chunk, 0)

        @pl.when(a > 0)
        def _():
            wait_from(xh.at[p, 0], xh_recv.at[p, 0])

        @pl.when(a < n_gx - 1)
        def _():
            wait_from(xh.at[p, 1], xh_recv.at[p, 1])

        @pl.when(b > 0)
        def _():
            wait_from(yh.at[p, 0], yh_recv.at[p, 0])

        @pl.when(b < n_gy - 1)
        def _():
            wait_from(yh.at[p, 1], yh_recv.at[p, 1])

        D[:, 0] = xh[p, 0]
        D[:, cx + 1] = xh[p, 1]
        row_i = lax.broadcasted_iota(jnp.int32, (cy, LANES), 0)
        lane_i = lax.broadcasted_iota(jnp.int32, (cy, LANES), 1)

        def lap_row(x):
            top = top_add[pl.ds(pl.multiple_of(x * cy, cy), cy), :]
            scale = A[x]
            for f in range(3):
                c = D[f, x + 1]
                lap = D[f, x] + D[f, x + 2] - 6.0 * c
                lap += jnp.where(row_i == 0, yh[p, 0, f, pl.ds(x, 1), :], pltpu.roll(c, 1, 0))
                lap += jnp.where(row_i == cy - 1, yh[p, 1, f, pl.ds(x, 1), :], pltpu.roll(c, cy - 1, 0))
                lap += jnp.where(lane_i == 0, 0.0, pltpu.roll(c, 1, 1))
                lap += jnp.where(lane_i == LANES - 1, 0.0, pltpu.roll(c, LANES - 1, 1))
                push = jnp.where(lane_i == LANES - 1, pltpu.roll(top, 2 - f, 1) if f < 2 else top, 0.0)
                v = V[f, x] + scale * lap + push
                V[f, x] = v
                base = pl.multiple_of(x * (cy * 8), cy * 8)
                flat[pl.ds(base + f, cy, stride=8), :] = c + TIME_STEP * v
                flat[pl.ds(base + 3 + f, cy, stride=8), :] = v

        def lap_rows(i, _):
            lap_row(2 * i)
            lap_row(2 * i + 1)
            return 0

        lax.fori_loop(0, cx // 8, lap_rows, 0)

        for k in range(1, n_gy):
            src = lax.rem(b + k, n_gy)
            wait_from(rx.at[p, src], m_recv.at[p, src])
        got = [rx[p, src] for src in range(n_gy)]
        replies = [jnp.zeros((8, LANES), F32) for _ in range(n_gy)]
        springs = []
        for j in range(n_blocks):
            rec = jnp.zeros((8, LANES), F32)
            for src in range(n_gy):
                moved = pltpu.roll(got[src], ((src - j) * group) % LANES, 1) if src != j else got[src]
                rec = jnp.where(lane // group == src, moved, rec)
            diff = [near[j, f] - rec[f:f + 1] for f in range(6)]
            gain = rec[6:7] / (1.0 + diff[0] * diff[0] + diff[1] * diff[1] + diff[2] * diff[2])
            force = jnp.zeros((8, LANES), F32)
            for f in range(3):
                spring = gain * (PARTICLE_K * diff[f])
                springs.append(spring)
                total = jnp.sum(spring + gain * (DRAG_COEF * diff[3 + f]), axis=0, keepdims=True)
                force = jnp.where(sub == f, total, force)
            force = force * (1.0 / n_nbr)
            for src in range(n_gy):
                moved = pltpu.roll(force, ((j - src) * group) % LANES, 1) if src != j else force
                replies[src] = jnp.where(lane // group == j, moved, replies[src])
        for src in range(n_gy):
            ans[src] = replies[src]
        ax[p, b] = ans[b]
        a_copies = []
        for k in range(1, n_gy):
            o = lax.rem(b + k, n_gy)
            a_copies.append(remote(ans.at[o], ax.at[p, b], a_send.at[k], a_recv.at[p, b], (a, o)))
            a_copies[-1].start()

        for j in range(n_blocks):
            parts = [two_parts(springs[3 * j + f]) for f in range(3)]
            lhs = jnp.concatenate([q[0] for q in parts] + [q[1] for q in parts], axis=0).astype(BF16)
            wide = dot_nt(lhs, nbr_hot[j])
            change = jnp.zeros((8, LANES), F32)
            for f in range(3):
                acc = jnp.zeros((8, LANES), F32)
                for k in range(n_nbr):
                    ks = slice(k * LANES, (k + 1) * LANES)
                    acc = jnp.where(sub == k, wide[8 * f:8 * f + 8, ks] + wide[24 + 8 * f:32 + 8 * f, ks], acc)
                total = jnp.sum(acc, axis=0, keepdims=True) * (-TIME_STEP / n_nbr)
                change = change + jnp.where(sub == 3 + f, total, 0.0)
            state = part[j] + change
            part[j] = state + jnp.where(sub < 3, TIME_STEP * pltpu.roll(state, 5, 0), 0.0)

        lax.fori_loop(cx // 8, cx // 2, lap_rows, 0)
        masses = [recs_buf[w, 6:7, :] for w in range(rec_tiles)]
        read_records(after)
        read_segments()

        for k in range(1, n_gy):
            src = lax.rem(b + k, n_gy)
            wait_from(ax.at[p, src], a_recv.at[p, src])
        own_row = owner_v[s, 0]
        rank_row = rank[pl.ds(s, 1), :]
        rows = []
        for w in range(rec_tiles):
            ws = slice(w * LANES, (w + 1) * LANES)
            own8, rank8 = rows8(own_row[:, ws]), rows8(rank_row[:, ws])
            force = jnp.zeros((8, LANES), F32)
            for o in range(n_gy):
                force = jnp.where(own8 == o, take_lanes(ax[p, o], rank8), force)
            hi, lo = two_parts(TIME_STEP * force / masses[w])
            push_buf[0, w] = hi
            push_buf[1, w] = lo
            rows.append(jnp.concatenate([hi, lo], axis=0))
        both = jnp.dot(jnp.concatenate(rows, axis=1).astype(BF16), match_hot[...], preferred_element_type=F32)
        more = both[:8] + both[8:]
        more = TIME_STEP * more + pltpu.roll(more, 3, 0)
        for copy in m_copies + a_copies + [p_copy]:
            copy.wait_send()
        for there, copy, _k in halos + y_halos:
            @pl.when(there)
            def _(copy=copy):
                copy.wait_send()
        for w in range(rec_tiles):
            recs_buf[w] = recs_buf[w] + more[:, w * LANES:(w + 1) * LANES]
        for w in range(seg_tiles):
            seg[w] = seg_pre[w] + more[:, n_rec + w * LANES:n_rec + (w + 1) * LANES]
        return 0

    lax.fori_loop(0, steps, step, 0)
    add_forces(steps - 1)
    out_d = pltpu.make_async_copy(D.at[:, pl.ds(1, cx)], disp_out, out_sem.at[0])
    out_v = pltpu.make_async_copy(V, vel_out, out_sem.at[1])
    out_d.start()
    out_v.start()
    out_d.wait()
    out_v.wait()


def local(n_gx, n_gy, disp, vel, stiff, mass, contact_cells, contact_match, eroded, owners, bpos, bvel, bnbr):
    cx, cy, nz = disp.shape[1:]
    steps, n_rec = eroded.shape[0], eroded.shape[3]
    n_seg = contact_cells.shape[2]
    n_slots = bpos.shape[3]
    n_blocks = n_slots // LANES
    n_nbr = bnbr.shape[2]
    dims = (n_gx, n_gy, cx, cy, steps, n_rec, n_seg, n_blocks, n_nbr)
    contact = contact_cells.reshape(1, n_seg)
    cells = eroded.reshape(steps, 1, 1, n_rec)
    vm = pl.BlockSpec(memory_space=pltpu.VMEM)
    sm = pl.BlockSpec(memory_space=pltpu.SMEM)
    anywhere = pl.BlockSpec(memory_space=pl.ANY)
    dma = pltpu.SemaphoreType.DMA
    tile = (8, LANES)
    return pl.pallas_call(
        functools.partial(kernel, dims),
        out_shape=(jax.ShapeDtypeStruct(disp.shape, F32), jax.ShapeDtypeStruct(vel.shape, F32)),
        in_specs=[sm, sm] + [anywhere] * 4 + [vm] * 7,
        out_specs=(anywhere, anywhere),
        scratch_shapes=[
            pltpu.VMEM((3, cx + 2, cy, nz), F32),
            pltpu.VMEM((3, cx, cy, nz), F32),
            pltpu.VMEM((cx, cy, nz), F32),
            pltpu.VMEM((cx, cy, nz), F32),
            pltpu.VMEM((cx * cy, 8, nz), F32),
            pltpu.VMEM((n_rec // LANES,) + tile, F32),
            pltpu.VMEM((n_seg // LANES,) + tile, F32),
            pltpu.VMEM((2, n_rec // LANES) + tile, F32),
            pltpu.VMEM((n_blocks, 6) + tile, F32),
            pltpu.VMEM((n_rec, n_rec + n_seg), BF16),
            pltpu.VMEM((steps, n_rec, LANES), F32),
            pltpu.VMEM((cx * cy, nz), F32),
            pltpu.VMEM((2, 3, cx, nz), F32),
            pltpu.VMEM((2, 2, 3, cx, nz), F32),
            pltpu.VMEM((2, 2, 3, cy, nz), F32),
            pltpu.VMEM((n_gy,) + tile, F32),
            pltpu.VMEM((2, n_gy) + tile, F32),
            pltpu.VMEM((n_gy,) + tile, F32),
            pltpu.VMEM((2, n_gy) + tile, F32),
            pltpu.VMEM((n_seg // LANES,) + tile, F32),
            pltpu.VMEM((2, n_seg // LANES) + tile, F32),
            pltpu.VMEM((steps, n_gy, LANES), jnp.int32),
            pltpu.VMEM((steps, n_rec), jnp.int32),
            pltpu.VMEM((n_blocks,) + tile, F32),
            pltpu.VMEM((n_blocks,) + tile, jnp.int32),
            pltpu.VMEM((n_blocks, n_nbr * LANES, LANES), BF16),
            pltpu.VMEM((cx * cy, n_seg), BF16),
            pltpu.VMEM((6 * LANES, n_rec), BF16),
            dma((2,)), dma((4,)),
            dma((2,)), dma((2, 2)),
            dma((2,)), dma((2, 2)),
            dma((n_gy,)), dma((2, n_gy)),
            dma((n_gy,)), dma((2, n_gy)),
            dma, dma((2,)),
        ],
        compiler_params=pltpu.CompilerParams(collective_id=0, has_side_effects=True, vmem_limit_bytes=60 * 2**20),
        name="dynamics",
    )(
        cells, contact, disp, vel, stiff, mass, contact, contact_match.reshape(1, n_seg), cells,
        owners.reshape(steps, 1, 1, n_rec), bpos[0, 0], bvel[0, 0], bnbr[0, 0],
    )


def solution(mesh):
    return jax.shard_map(
        functools.partial(local, mesh.shape["gx"], mesh.shape["gy"]),
        mesh=mesh,
        in_specs=(
            P(None, "gx", "gy", None),
            P(None, "gx", "gy", None),
            P("gx", "gy", None),
            P("gx", "gy", None),
            P("gx", "gy", None),
            P("gx", "gy", None),
            P(None, "gx", "gy", None),
            P(None, "gx", "gy", None, None),
            P("gx", "gy", None, None),
            P("gx", "gy", None, None),
            P("gx", "gy", None, None),
        ),
        out_specs=(P(None, "gx", "gy", None), P(None, "gx", "gy", None)),
        check_vma=False,
    )
```

```python
import functools

import jax
import jax.numpy as jnp
from jax import lax
from jax.experimental import pallas as pl
from jax.experimental.pallas import tpu as pltpu
from jax.sharding import PartitionSpec as P

TIME_STEP = 0.2
CONTACT_K = 0.5
PARTICLE_K = 1.0
DRAG_COEF = 0.5
LANES = 128
F32 = jnp.float32
BF16 = jnp.bfloat16
MESH = pl.DeviceIdType.MESH


def take_lanes(x, idx):
    return jnp.take_along_axis(x, idx, axis=1, mode="promise_in_bounds")


def dot_nt(a, b):
    return lax.dot_general(a, b, (((1,), (1,)), ((), ())), preferred_element_type=F32)


def two_parts(x):
    hi = x.astype(BF16).astype(F32)
    return hi, x - hi


def rows8(row):
    return jnp.broadcast_to(row, (8, row.shape[1]))


def kernel(
    dims,
    cells_s, contact_s, disp_in, vel_in, stiff_in, mass_in, contact_v, match_v, cells_v, owner_v, bpos, bvel, bnbr,
    disp_out, vel_out,
    D, V, A, M, G, recs_buf, seg_pre, push_buf, near, match_hot, cell_col, top_add, ye, yh, xh, msg, rx, ans, ax, seg, ps, inv, rank, part, nbr, nbr_hot, seg_hot, b_both,
    out_sem, in_sem, ye_send, yh_recv, xe_send, xh_recv, m_send, m_recv, a_send, a_recv, p_send, p_recv,
):
    n_gx, n_gy, cx, cy, steps, n_rec, n_seg, n_blocks, n_nbr = dims
    n_cols = cx * cy
    group = LANES // n_gy
    rec_tiles = n_rec // LANES
    seg_tiles = n_seg // LANES
    chunk_x = 8
    chunk = chunk_x * cy
    a = lax.axis_index("gx")
    b = lax.axis_index("gy")
    mate = a + 1 - 2 * lax.rem(a, 2)
    lane = lax.broadcasted_iota(jnp.int32, (8, LANES), 1)
    sub = lax.broadcasted_iota(jnp.int32, (8, LANES), 0)

    flat = G.reshape(n_cols * 8, LANES)
    core = pl.ds(8, cy)

    loads = [
        pltpu.make_async_copy(disp_in, D.at[:, pl.ds(1, cx), core], in_sem.at[0]),
        pltpu.make_async_copy(vel_in, V, in_sem.at[1]),
        pltpu.make_async_copy(stiff_in, A, in_sem.at[2]),
        pltpu.make_async_copy(mass_in, M, in_sem.at[3]),
    ]
    for load in loads:
        load.start()
    yh[...] = jnp.zeros_like(yh)
    xh[...] = jnp.zeros_like(xh)
    push_buf[...] = jnp.zeros_like(push_buf)


    tri = jnp.where(
        lax.broadcasted_iota(jnp.int32, (n_rec, n_rec), 1) <= lax.broadcasted_iota(jnp.int32, (n_rec, n_rec), 0), 1.0, 0.0
    ).astype(BF16)

    def init_step(s, _):
        own = owner_v[s, 0]
        mine = lax.broadcasted_iota(jnp.int32, (n_gy, n_rec), 0) == own
        hot = jnp.where(mine, 1.0, 0.0)
        counted = dot_nt(jnp.concatenate([hot] * 2, axis=0).astype(BF16), tri)[:n_gy]
        rk = (jnp.sum(hot * counted, axis=0, keepdims=True) - 1.0).astype(jnp.int32)
        rank[pl.ds(s, 1), :] = rk
        rec = lax.broadcasted_iota(jnp.int32, (n_gy, n_rec), 1) + 1
        lo = jnp.where(mine, (rec & 127).astype(F32), 0.0)
        hi = jnp.where(mine, (rec >> 7).astype(F32), 0.0)
        q_hot = jnp.where(lax.broadcasted_iota(jnp.int32, (LANES, n_rec), 0) == rk, 1.0, 0.0).astype(BF16)
        both = dot_nt(jnp.concatenate([lo, hi], axis=0).astype(BF16), q_hot)
        inv[s] = (both[:n_gy] + 128.0 * both[n_gy:]).astype(jnp.int32) - 1
        cell_row = cells_v[s, 0].astype(F32)
        for w in range(rec_tiles):
            ws = slice(w * LANES, (w + 1) * LANES)
            cell_col[s, ws, :] = jnp.broadcast_to(cell_row[:, ws], (LANES, LANES)).T
        return 0

    lax.fori_loop(0, steps, init_step, 0)

    perm = lax.rem(lane, group) * n_gy + lane // group
    nrow = lax.broadcasted_iota(jnp.int32, (LANES, LANES), 0)

    def init_block(j, _):
        at = pl.ds(pl.multiple_of(j * LANES, LANES), LANES)
        rows = jnp.concatenate([bpos[:, at], bvel[:, at], jnp.zeros((2, LANES), F32)], axis=0)
        part[j] = take_lanes(rows, perm)
        old = take_lanes(bnbr[:, at], perm)
        new = lax.rem(old, n_gy) * group + old // n_gy
        nbr[j] = new
        for k in range(n_nbr):
            nbr_hot[j, :, k * LANES:(k + 1) * LANES] = jnp.where(nrow == new[k:k + 1], 1.0, 0.0).T.astype(BF16)
        return 0

    lax.fori_loop(0, n_blocks, init_block, 0)

    for load in loads:
        load.wait()

    def init_chunk(i, _):
        x0 = i * chunk_x
        xs = pl.ds(x0, chunk_x)
        m = M[xs].reshape(chunk, LANES)
        A[xs] = TIME_STEP * A[xs] / M[xs]
        base = pl.multiple_of(i * (chunk * 8), chunk * 8)
        for f in range(3):
            d = D[f, pl.ds(x0 + 1, chunk_x), core]
            v = V[f, xs]
            flat[pl.ds(base + f, chunk, stride=8), :] = d.reshape(chunk, LANES)
            flat[pl.ds(base + 3 + f, chunk, stride=8), :] = v.reshape(chunk, LANES)
            for xx in range(chunk_x):
                ye[0, f, pl.ds(x0 + xx, 1), :] = d[xx, 0:1]
                ye[1, f, pl.ds(x0 + xx, 1), :] = d[xx, cy - 1:cy]
        flat[pl.ds(base + 6, chunk, stride=8), :] = m
        flat[pl.ds(base + 7, chunk, stride=8), :] = jnp.zeros_like(m)
        cols = lax.broadcasted_iota(jnp.int32, (chunk, n_seg), 0) + i * chunk
        seg_hot[pl.ds(pl.multiple_of(i * chunk, chunk), chunk), :] = jnp.where(cols == contact_v[...], 1.0, 0.0).astype(BF16)
        return 0

    lax.fori_loop(0, cx // chunk_x, init_chunk, 0)

    barrier = pltpu.get_barrier_semaphore()
    for k in range(1, n_gy):
        pl.semaphore_signal(barrier, inc=1, device_id=(a, lax.rem(b + k, n_gy)), device_id_type=MESH)

    @pl.when(a > 0)
    def _():
        pl.semaphore_signal(barrier, inc=1, device_id=(a - 1, b), device_id_type=MESH)

    @pl.when(a < n_gx - 1)
    def _():
        pl.semaphore_signal(barrier, inc=1, device_id=(a + 1, b), device_id_type=MESH)

    n_near = jnp.where(a > 0, 1, 0) + jnp.where(a < n_gx - 1, 1, 0)
    pl.semaphore_wait(barrier, n_gy - 1 + n_near)

    def remote(src, dst, send, recv, to):
        return pltpu.make_async_remote_copy(src_ref=src, dst_ref=dst, send_sem=send, recv_sem=recv, device_id=to, device_id_type=MESH)

    def read_records(s):
        def read_rec(w, _):
            acc = jnp.zeros((8, LANES), F32)
            for t in range(LANES):
                cell = cells_s[s, 0, 0, w * LANES + t]
                acc = jnp.where(lane == t, take_lanes(G[cell >> 7], jnp.full((8, LANES), cell & 127, jnp.int32)), acc)
            recs_buf[w] = acc
            return 0

        lax.fori_loop(0, rec_tiles, read_rec, 0)

    def read_segments():
        def read_seg(w, _):
            acc = jnp.zeros((8, LANES), F32)
            for t in range(LANES):
                acc = jnp.where(lane == t, pltpu.roll(G[contact_s[0, w * LANES + t]], (t + 1) % LANES, 1), acc)
            seg_pre[w] = acc
            return 0

        lax.fori_loop(0, seg_tiles, read_seg, 0)

    def add_forces(s):
        cell_row = cells_v[s, 0]
        col_row = cell_row >> 7
        zrow = lax.broadcasted_iota(jnp.int32, (LANES, LANES), 0)
        for w in range(rec_tiles):
            ws = slice(w * LANES, (w + 1) * LANES)
            here = zrow == (cell_row[:, ws] & 127)
            for f in range(3):
                for q in range(2):
                    b_both[(2 * f + q) * LANES:(2 * f + q + 1) * LANES, ws] = jnp.where(
                        here, push_buf[q, w, f:f + 1, :], 0.0
                    ).astype(BF16)

        add_x = cx // 2
        add_n = add_x * cy

        def add_chunk(i, _):
            x0 = i * add_x
            cols = lax.broadcasted_iota(jnp.int32, (add_n, n_rec), 0) + i * add_n
            hot = jnp.where(cols == col_row, 1.0, 0.0).astype(BF16)
            for f in range(3):
                both = dot_nt(hot, b_both[pl.ds(2 * f * LANES, 2 * LANES), :])
                add = both[:, :LANES] + both[:, LANES:]
                v = V[f, pl.ds(x0, add_x)].reshape(add_n, LANES) + add
                d = D[f, pl.ds(x0 + 1, add_x), core].reshape(add_n, LANES) + TIME_STEP * v
                V[f, pl.ds(x0, add_x)] = v.reshape(add_x, cy, LANES)
                D[f, pl.ds(x0 + 1, add_x), core] = d.reshape(add_x, cy, LANES)
                for xx in range(add_x):
                    ye[0, f, pl.ds(x0 + xx, 1), :] = d[xx * cy:xx * cy + 1]
                    ye[1, f, pl.ds(x0 + xx, 1), :] = d[xx * cy + cy - 1:xx * cy + cy]
            return 0

        lax.fori_loop(0, cx // add_x, add_chunk, 0)

    read_records(0)
    read_segments()
    for w in range(seg_tiles):
        seg[w] = seg_pre[w]

    def step(s, _):
        p = lax.rem(s, 2)
        after = jnp.minimum(s + 1, steps - 1)
        halos = (
            (a > 0, remote(D.at[:, 1, core], xh.at[p, 1], xe_send.at[0], xh_recv.at[p, 1], (a - 1, b)), 0),
            (a < n_gx - 1, remote(D.at[:, cx, core], xh.at[p, 0], xe_send.at[1], xh_recv.at[p, 0], (a + 1, b)), 1),
        )
        y_halos = (
            (b > 0, remote(ye.at[0], yh.at[p, 1], ye_send.at[0], yh_recv.at[p, 1], (a, b - 1)), 0),
            (b < n_gy - 1, remote(ye.at[1], yh.at[p, 0], ye_send.at[1], yh_recv.at[p, 0], (a, b + 1)), 1),
        )

        def wait_from(dst, recv):
            pltpu.make_async_copy(dst, dst, recv).wait()

        recs = [recs_buf[w] for w in range(rec_tiles)]
        for o in range(n_gy):
            idx = rows8(inv[s, o:o + 1, :])
            out = jnp.zeros((8, LANES), F32)
            for w in range(rec_tiles):
                out = jnp.where((idx >> 7) == w, take_lanes(recs[w], idx & 127), out)
            msg[o] = out
        rx[p, b] = msg[b]
        m_copies = []
        for k in range(1, n_gy):
            o = lax.rem(b + k, n_gy)
            m_copies.append(remote(msg.at[o], rx.at[p, b], m_send.at[k], m_recv.at[p, b], (a, o)))
            m_copies[-1].start()
        p_copy = remote(seg, ps.at[p], p_send, p_recv.at[p], (mate, b))
        p_copy.start()

        @pl.when(s > 0)
        def _():
            add_forces(s - 1)

        for there, copy, _k in halos + y_halos:
            @pl.when(there)
            def _(copy=copy):
                copy.start()

        goal = jnp.concatenate([cells_v[after, 0], contact_v[...] * LANES + (LANES - 1)], axis=1).astype(F32)

        def match_tile(w, _):
            at = pl.ds(pl.multiple_of(w * LANES, LANES), LANES)
            col = cell_col[s, at, :]
            for t in range(rec_tiles + seg_tiles):
                ts = slice(t * LANES, (t + 1) * LANES)
                match_hot[at, ts] = jnp.where(col == goal[:, ts], 1.0, 0.0).astype(BF16)
            return 0

        lax.fori_loop(0, rec_tiles, match_tile, 0)
        for j in range(n_blocks):
            state = part[j]
            idx = nbr[j]
            for f in range(6):
                near[j, f] = take_lanes(rows8(state[f:f + 1]), idx)

        wait_from(ps.at[p], p_recv.at[p])
        c_parts = [[], []]
        for w in range(seg_tiles):
            idx = rows8(match_v[:, w * LANES:(w + 1) * LANES])
            facing = jnp.zeros((8, LANES), F32)
            for u in range(seg_tiles):
                facing = jnp.where((idx >> 7) == u, take_lanes(ps[p, u], idx & 127), facing)
            own = seg[w]
            pull = (TIME_STEP * CONTACT_K) * (facing - own) / own[6:7]
            hi, lo = two_parts(pltpu.roll(jnp.where(sub < 3, pull, 0.0), 5, 0))
            c_parts[0].append(hi)
            c_parts[1].append(lo)
        zero_rows = jnp.zeros((LANES - 8, n_seg), F32)
        c_mat = jnp.concatenate(
            [zero_rows, jnp.concatenate(c_parts[0], axis=1), zero_rows, jnp.concatenate(c_parts[1], axis=1)], axis=0
        ).astype(BF16)

        def top_chunk(i, _):
            at = pl.ds(pl.multiple_of(i * chunk, chunk), chunk)
            hot = seg_hot[at, :]
            both = dot_nt(hot, c_mat)
            top_add[at, :] = both[:, :LANES] + both[:, LANES:]
            return 0

        lax.fori_loop(0, cx // chunk_x, top_chunk, 0)

        @pl.when(a > 0)
        def _():
            wait_from(xh.at[p, 0], xh_recv.at[p, 0])

        @pl.when(a < n_gx - 1)
        def _():
            wait_from(xh.at[p, 1], xh_recv.at[p, 1])

        @pl.when(b > 0)
        def _():
            wait_from(yh.at[p, 0], yh_recv.at[p, 0])

        @pl.when(b < n_gy - 1)
        def _():
            wait_from(yh.at[p, 1], yh_recv.at[p, 1])

        D[:, 0, core] = xh[p, 0]
        D[:, cx + 1, core] = xh[p, 1]

        def y_rows(i, _):
            for u in range(8):
                x = i * 8 + u
                for f in range(3):
                    D[f, x + 1, pl.ds(7, 1), :] = yh[p, 0, f, pl.ds(x, 1), :]
                    D[f, x + 1, pl.ds(8 + cy, 1), :] = yh[p, 1, f, pl.ds(x, 1), :]
            return 0

        lax.fori_loop(0, cx // 8, y_rows, 0)

        lane_i = lax.broadcasted_iota(jnp.int32, (cy, LANES), 1)

        def lap_row(x):
            top = top_add[pl.ds(pl.multiple_of(x * cy, cy), cy), :]
            scale = A[x]
            for f in range(3):
                c = D[f, x + 1, core]
                lap = D[f, x, core] + D[f, x + 2, core] - 6.0 * c
                lap += D[f, x + 1, pl.ds(7, cy)] + D[f, x + 1, pl.ds(9, cy)]
                lap += jnp.where(lane_i == 0, 0.0, pltpu.roll(c, 1, 1))
                lap += jnp.where(lane_i == LANES - 1, 0.0, pltpu.roll(c, LANES - 1, 1))
                push = jnp.where(lane_i == LANES - 1, pltpu.roll(top, 2 - f, 1) if f < 2 else top, 0.0)
                v = V[f, x] + scale * lap + push
                V[f, x] = v
                base = pl.multiple_of(x * (cy * 8), cy * 8)
                flat[pl.ds(base + f, cy, stride=8), :] = c + TIME_STEP * v
                flat[pl.ds(base + 3 + f, cy, stride=8), :] = v

        def lap_rows(i, _):
            for u in range(4):
                lap_row(4 * i + u)
            return 0

        lax.fori_loop(0, cx // 16, lap_rows, 0)

        for k in range(1, n_gy):
            src = lax.rem(b + k, n_gy)
            wait_from(rx.at[p, src], m_recv.at[p, src])
        got = [rx[p, src] for src in range(n_gy)]
        replies = [jnp.zeros((8, LANES), F32) for _ in range(n_gy)]
        springs = []
        for j in range(n_blocks):
            rec = jnp.zeros((8, LANES), F32)
            for src in range(n_gy):
                moved = pltpu.roll(got[src], ((src - j) * group) % LANES, 1) if src != j else got[src]
                rec = jnp.where(lane // group == src, moved, rec)
            diff = [near[j, f] - rec[f:f + 1] for f in range(6)]
            gain = rec[6:7] / (1.0 + diff[0] * diff[0] + diff[1] * diff[1] + diff[2] * diff[2])
            force = jnp.zeros((8, LANES), F32)
            for f in range(3):
                spring = gain * (PARTICLE_K * diff[f])
                springs.append(spring)
                total = jnp.sum(spring + gain * (DRAG_COEF * diff[3 + f]), axis=0, keepdims=True)
                force = jnp.where(sub == f, total, force)
            force = force * (1.0 / n_nbr)
            for src in range(n_gy):
                moved = pltpu.roll(force, ((j - src) * group) % LANES, 1) if src != j else force
                replies[src] = jnp.where(lane // group == j, moved, replies[src])
        for src in range(n_gy):
            ans[src] = replies[src]
        ax[p, b] = ans[b]
        a_copies = []
        for k in range(1, n_gy):
            o = lax.rem(b + k, n_gy)
            a_copies.append(remote(ans.at[o], ax.at[p, b], a_send.at[k], a_recv.at[p, b], (a, o)))
            a_copies[-1].start()

        for j in range(n_blocks):
            parts = [two_parts(springs[3 * j + f]) for f in range(3)]
            lhs = jnp.concatenate([q[0] for q in parts] + [q[1] for q in parts], axis=0).astype(BF16)
            wide = jnp.dot(lhs, nbr_hot[j], preferred_element_type=F32)
            change = jnp.zeros((8, LANES), F32)
            for f in range(3):
                acc = jnp.zeros((8, LANES), F32)
                for k in range(n_nbr):
                    ks = slice(k * LANES, (k + 1) * LANES)
                    acc = jnp.where(sub == k, wide[8 * f:8 * f + 8, ks] + wide[24 + 8 * f:32 + 8 * f, ks], acc)
                total = jnp.sum(acc, axis=0, keepdims=True) * (-TIME_STEP / n_nbr)
                change = change + jnp.where(sub == 3 + f, total, 0.0)
            state = part[j] + change
            part[j] = state + jnp.where(sub < 3, TIME_STEP * pltpu.roll(state, 5, 0), 0.0)

        lax.fori_loop(cx // 16, cx // 4, lap_rows, 0)
        masses = [recs_buf[w, 6:7, :] for w in range(rec_tiles)]
        read_records(after)
        read_segments()

        for k in range(1, n_gy):
            src = lax.rem(b + k, n_gy)
            wait_from(ax.at[p, src], a_recv.at[p, src])
        own_row = owner_v[s, 0]
        rank_row = rank[pl.ds(s, 1), :]
        rows = []
        for w in range(rec_tiles):
            ws = slice(w * LANES, (w + 1) * LANES)
            own8, rank8 = rows8(own_row[:, ws]), rows8(rank_row[:, ws])
            force = jnp.zeros((8, LANES), F32)
            for o in range(n_gy):
                force = jnp.where(own8 == o, take_lanes(ax[p, o], rank8), force)
            hi, lo = two_parts(TIME_STEP * force / masses[w])
            push_buf[0, w] = hi
            push_buf[1, w] = lo
            rows.append(jnp.concatenate([hi, lo], axis=0))
        both = jnp.dot(jnp.concatenate(rows, axis=1).astype(BF16), match_hot[...], preferred_element_type=F32)
        more = both[:8] + both[8:]
        more = TIME_STEP * more + pltpu.roll(more, 3, 0)
        for copy in m_copies + a_copies + [p_copy]:
            copy.wait_send()
        for there, copy, _k in halos + y_halos:
            @pl.when(there)
            def _(copy=copy):
                copy.wait_send()
        for w in range(rec_tiles):
            recs_buf[w] = recs_buf[w] + more[:, w * LANES:(w + 1) * LANES]
        for w in range(seg_tiles):
            seg[w] = seg_pre[w] + more[:, n_rec + w * LANES:n_rec + (w + 1) * LANES]
        return 0

    lax.fori_loop(0, steps, step, 0)
    add_forces(steps - 1)
    out_d = pltpu.make_async_copy(D.at[:, pl.ds(1, cx), core], disp_out, out_sem.at[0])
    out_v = pltpu.make_async_copy(V, vel_out, out_sem.at[1])
    out_d.start()
    out_v.start()
    out_d.wait()
    out_v.wait()


def local(n_gx, n_gy, disp, vel, stiff, mass, contact_cells, contact_match, eroded, owners, bpos, bvel, bnbr):
    cx, cy, nz = disp.shape[1:]
    steps, n_rec = eroded.shape[0], eroded.shape[3]
    n_seg = contact_cells.shape[2]
    n_slots = bpos.shape[3]
    n_blocks = n_slots // LANES
    n_nbr = bnbr.shape[2]
    dims = (n_gx, n_gy, cx, cy, steps, n_rec, n_seg, n_blocks, n_nbr)
    contact = contact_cells.reshape(1, n_seg)
    cells = eroded.reshape(steps, 1, 1, n_rec)
    vm = pl.BlockSpec(memory_space=pltpu.VMEM)
    sm = pl.BlockSpec(memory_space=pltpu.SMEM)
    anywhere = pl.BlockSpec(memory_space=pl.ANY)
    dma = pltpu.SemaphoreType.DMA
    tile = (8, LANES)
    return pl.pallas_call(
        functools.partial(kernel, dims),
        out_shape=(jax.ShapeDtypeStruct(disp.shape, F32), jax.ShapeDtypeStruct(vel.shape, F32)),
        in_specs=[sm, sm] + [anywhere] * 4 + [vm] * 7,
        out_specs=(anywhere, anywhere),
        scratch_shapes=[
            pltpu.VMEM((3, cx + 2, cy + 16, nz), F32),
            pltpu.VMEM((3, cx, cy, nz), F32),
            pltpu.VMEM((cx, cy, nz), F32),
            pltpu.VMEM((cx, cy, nz), F32),
            pltpu.VMEM((cx * cy, 8, nz), F32),
            pltpu.VMEM((n_rec // LANES,) + tile, F32),
            pltpu.VMEM((n_seg // LANES,) + tile, F32),
            pltpu.VMEM((2, n_rec // LANES) + tile, F32),
            pltpu.VMEM((n_blocks, 6) + tile, F32),
            pltpu.VMEM((n_rec, n_rec + n_seg), BF16),
            pltpu.VMEM((steps, n_rec, LANES), F32),
            pltpu.VMEM((cx * cy, nz), F32),
            pltpu.VMEM((2, 3, cx, nz), F32),
            pltpu.VMEM((2, 2, 3, cx, nz), F32),
            pltpu.VMEM((2, 2, 3, cy, nz), F32),
            pltpu.VMEM((n_gy,) + tile, F32),
            pltpu.VMEM((2, n_gy) + tile, F32),
            pltpu.VMEM((n_gy,) + tile, F32),
            pltpu.VMEM((2, n_gy) + tile, F32),
            pltpu.VMEM((n_seg // LANES,) + tile, F32),
            pltpu.VMEM((2, n_seg // LANES) + tile, F32),
            pltpu.VMEM((steps, n_gy, LANES), jnp.int32),
            pltpu.VMEM((steps, n_rec), jnp.int32),
            pltpu.VMEM((n_blocks,) + tile, F32),
            pltpu.VMEM((n_blocks,) + tile, jnp.int32),
            pltpu.VMEM((n_blocks, LANES, n_nbr * LANES), BF16),
            pltpu.VMEM((cx * cy, n_seg), BF16),
            pltpu.VMEM((6 * LANES, n_rec), BF16),
            dma((2,)), dma((4,)),
            dma((2,)), dma((2, 2)),
            dma((2,)), dma((2, 2)),
            dma((n_gy,)), dma((2, n_gy)),
            dma((n_gy,)), dma((2, n_gy)),
            dma, dma((2,)),
        ],
        compiler_params=pltpu.CompilerParams(collective_id=0, has_side_effects=True, vmem_limit_bytes=60 * 2**20),
        name="dynamics",
    )(
        cells, contact, disp, vel, stiff, mass, contact, contact_match.reshape(1, n_seg), cells,
        owners.reshape(steps, 1, 1, n_rec), bpos[0, 0], bvel[0, 0], bnbr[0, 0],
    )


def solution(mesh):
    return jax.shard_map(
        functools.partial(local, mesh.shape["gx"], mesh.shape["gy"]),
        mesh=mesh,
        in_specs=(
            P(None, "gx", "gy", None),
            P(None, "gx", "gy", None),
            P("gx", "gy", None),
            P("gx", "gy", None),
            P("gx", "gy", None),
            P("gx", "gy", None),
            P(None, "gx", "gy", None),
            P(None, "gx", "gy", None, None),
            P("gx", "gy", None, None),
            P("gx", "gy", None, None),
            P("gx", "gy", None, None),
        ),
        out_specs=(P(None, "gx", "gy", None), P(None, "gx", "gy", None)),
        check_vma=False,
    )
```

```python
import functools

import jax
import jax.numpy as jnp
from jax import lax
from jax.experimental import pallas as pl
from jax.experimental.pallas import tpu as pltpu
from jax.sharding import PartitionSpec as P

TIME_STEP = 0.2
CONTACT_K = 0.5
PARTICLE_K = 1.0
DRAG_COEF = 0.5
LANES = 128
F32 = jnp.float32
BF16 = jnp.bfloat16
MESH = pl.DeviceIdType.MESH


def take_lanes(x, idx):
    return jnp.take_along_axis(x, idx, axis=1, mode="promise_in_bounds")


def dot_nt(a, b):
    return lax.dot_general(a, b, (((1,), (1,)), ((), ())), preferred_element_type=F32)


def two_parts(x):
    hi = x.astype(BF16).astype(F32)
    return hi, x - hi


def rows8(row):
    return jnp.broadcast_to(row, (8, row.shape[1]))


def kernel(
    dims,
    cells_s, contact_s, disp_in, vel_in, stiff_in, mass_in, contact_v, match_v, cells_v, owner_v, bpos, bvel, bnbr,
    disp_out, vel_out,
    D, V, A, M, G, recs_buf, seg_pre, push_buf, near, match_hot, cell_col, top_add, ye, yh, xh, msg, rx, ans, ax, seg, ps, inv, rank, part, nbr, nbr_hot, seg_hot, b_both,
    out_sem, in_sem, ye_send, yh_recv, xe_send, xh_recv, m_send, m_recv, a_send, a_recv, p_send, p_recv,
):
    n_gx, n_gy, cx, cy, steps, n_rec, n_seg, n_blocks, n_nbr = dims
    n_cols = cx * cy
    group = LANES // n_gy
    rec_tiles = n_rec // LANES
    seg_tiles = n_seg // LANES
    chunk_x = 8
    chunk = chunk_x * cy
    a = lax.axis_index("gx")
    b = lax.axis_index("gy")
    mate = a + 1 - 2 * lax.rem(a, 2)
    lane = lax.broadcasted_iota(jnp.int32, (8, LANES), 1)
    sub = lax.broadcasted_iota(jnp.int32, (8, LANES), 0)

    flat = G.reshape(n_cols * 8, LANES)
    core = pl.ds(8, cy)

    loads = [
        pltpu.make_async_copy(disp_in, D.at[:, pl.ds(1, cx), core], in_sem.at[0]),
        pltpu.make_async_copy(vel_in, V, in_sem.at[1]),
        pltpu.make_async_copy(stiff_in, A, in_sem.at[2]),
        pltpu.make_async_copy(mass_in, M, in_sem.at[3]),
    ]
    for load in loads:
        load.start()
    yh[...] = jnp.zeros_like(yh)
    xh[...] = jnp.zeros_like(xh)
    push_buf[...] = jnp.zeros_like(push_buf)


    tri = jnp.where(
        lax.broadcasted_iota(jnp.int32, (n_rec, n_rec), 1) <= lax.broadcasted_iota(jnp.int32, (n_rec, n_rec), 0), 1.0, 0.0
    ).astype(BF16)

    def init_step(s, _):
        own = owner_v[s, 0]
        mine = lax.broadcasted_iota(jnp.int32, (n_gy, n_rec), 0) == own
        hot = jnp.where(mine, 1.0, 0.0)
        counted = dot_nt(jnp.concatenate([hot] * 2, axis=0).astype(BF16), tri)[:n_gy]
        rk = (jnp.sum(hot * counted, axis=0, keepdims=True) - 1.0).astype(jnp.int32)
        rank[pl.ds(s, 1), :] = rk
        rec = lax.broadcasted_iota(jnp.int32, (n_gy, n_rec), 1) + 1
        lo = jnp.where(mine, (rec & 127).astype(F32), 0.0)
        hi = jnp.where(mine, (rec >> 7).astype(F32), 0.0)
        q_hot = jnp.where(lax.broadcasted_iota(jnp.int32, (LANES, n_rec), 0) == rk, 1.0, 0.0).astype(BF16)
        both = dot_nt(jnp.concatenate([lo, hi], axis=0).astype(BF16), q_hot)
        inv[s] = (both[:n_gy] + 128.0 * both[n_gy:]).astype(jnp.int32) - 1
        cell_row = cells_v[s, 0].astype(F32)
        for w in range(rec_tiles):
            ws = slice(w * LANES, (w + 1) * LANES)
            cell_col[s, ws, :] = jnp.broadcast_to(cell_row[:, ws], (LANES, LANES)).T
        return 0

    lax.fori_loop(0, steps, init_step, 0)

    perm = lax.rem(lane, group) * n_gy + lane // group
    nrow = lax.broadcasted_iota(jnp.int32, (LANES, LANES), 0)

    def init_block(j, _):
        at = pl.ds(pl.multiple_of(j * LANES, LANES), LANES)
        rows = jnp.concatenate([bpos[f, 0, :, at] for f in range(3)] + [bvel[f, 0, :, at] for f in range(3)] + [jnp.zeros((2, LANES), F32)], axis=0)
        part[j] = take_lanes(rows, perm)
        old = take_lanes(bnbr[0, 0, :, at], perm)
        new = lax.rem(old, n_gy) * group + old // n_gy
        nbr[j] = new
        for k in range(n_nbr):
            nbr_hot[j, :, k * LANES:(k + 1) * LANES] = jnp.where(nrow == new[k:k + 1], 1.0, 0.0).T.astype(BF16)
        return 0

    lax.fori_loop(0, n_blocks, init_block, 0)

    for load in loads:
        load.wait()

    def init_chunk(i, _):
        x0 = i * chunk_x
        xs = pl.ds(x0, chunk_x)
        m = M[xs].reshape(chunk, LANES)
        A[xs] = TIME_STEP * A[xs] / M[xs]
        base = pl.multiple_of(i * (chunk * 8), chunk * 8)
        for f in range(3):
            d = D[f, pl.ds(x0 + 1, chunk_x), core]
            v = V[f, xs]
            flat[pl.ds(base + f, chunk, stride=8), :] = d.reshape(chunk, LANES)
            flat[pl.ds(base + 3 + f, chunk, stride=8), :] = v.reshape(chunk, LANES)
            for xx in range(chunk_x):
                ye[0, f, pl.ds(x0 + xx, 1), :] = d[xx, 0:1]
                ye[1, f, pl.ds(x0 + xx, 1), :] = d[xx, cy - 1:cy]
        flat[pl.ds(base + 6, chunk, stride=8), :] = m
        flat[pl.ds(base + 7, chunk, stride=8), :] = jnp.zeros_like(m)
        cols = lax.broadcasted_iota(jnp.int32, (chunk, n_seg), 0) + i * chunk
        seg_hot[pl.ds(pl.multiple_of(i * chunk, chunk), chunk), :] = jnp.where(cols == contact_v[...], 1.0, 0.0).astype(BF16)
        return 0

    lax.fori_loop(0, cx // chunk_x, init_chunk, 0)

    barrier = pltpu.get_barrier_semaphore()
    for k in range(1, n_gy):
        pl.semaphore_signal(barrier, inc=1, device_id=(a, lax.rem(b + k, n_gy)), device_id_type=MESH)

    @pl.when(a > 0)
    def _():
        pl.semaphore_signal(barrier, inc=1, device_id=(a - 1, b), device_id_type=MESH)

    @pl.when(a < n_gx - 1)
    def _():
        pl.semaphore_signal(barrier, inc=1, device_id=(a + 1, b), device_id_type=MESH)

    n_near = jnp.where(a > 0, 1, 0) + jnp.where(a < n_gx - 1, 1, 0)
    pl.semaphore_wait(barrier, n_gy - 1 + n_near)

    def remote(src, dst, send, recv, to):
        return pltpu.make_async_remote_copy(src_ref=src, dst_ref=dst, send_sem=send, recv_sem=recv, device_id=to, device_id_type=MESH)

    def read_records(s):
        def read_rec(w, _):
            acc = jnp.zeros((8, LANES), F32)
            for t in range(LANES):
                cell = cells_s[s, 0, 0, w * LANES + t]
                acc = jnp.where(lane == t, take_lanes(G[cell >> 7], jnp.full((8, LANES), cell & 127, jnp.int32)), acc)
            recs_buf[w] = acc
            return 0

        lax.fori_loop(0, rec_tiles, read_rec, 0)

    def read_segments():
        def read_seg(w, _):
            acc = jnp.zeros((8, LANES), F32)
            for t in range(LANES):
                acc = jnp.where(lane == t, pltpu.roll(G[contact_s[0, w * LANES + t]], (t + 1) % LANES, 1), acc)
            seg_pre[w] = acc
            return 0

        lax.fori_loop(0, seg_tiles, read_seg, 0)

    def add_forces(s):
        cell_row = cells_v[s, 0]
        col_row = cell_row >> 7
        zrow = lax.broadcasted_iota(jnp.int32, (LANES, LANES), 0)
        for w in range(rec_tiles):
            ws = slice(w * LANES, (w + 1) * LANES)
            here = zrow == (cell_row[:, ws] & 127)
            for f in range(3):
                for q in range(2):
                    b_both[(2 * f + q) * LANES:(2 * f + q + 1) * LANES, ws] = jnp.where(
                        here, push_buf[q, w, f:f + 1, :], 0.0
                    ).astype(BF16)

        add_x = cx // 2
        add_n = add_x * cy

        def add_chunk(i, _):
            x0 = i * add_x
            cols = lax.broadcasted_iota(jnp.int32, (add_n, n_rec), 0) + i * add_n
            hot = jnp.where(cols == col_row, 1.0, 0.0).astype(BF16)
            for f in range(3):
                both = dot_nt(hot, b_both[pl.ds(2 * f * LANES, 2 * LANES), :])
                add = both[:, :LANES] + both[:, LANES:]
                v = V[f, pl.ds(x0, add_x)].reshape(add_n, LANES) + add
                d = D[f, pl.ds(x0 + 1, add_x), core].reshape(add_n, LANES) + TIME_STEP * v
                V[f, pl.ds(x0, add_x)] = v.reshape(add_x, cy, LANES)
                D[f, pl.ds(x0 + 1, add_x), core] = d.reshape(add_x, cy, LANES)
                for xx in range(add_x):
                    ye[0, f, pl.ds(x0 + xx, 1), :] = d[xx * cy:xx * cy + 1]
                    ye[1, f, pl.ds(x0 + xx, 1), :] = d[xx * cy + cy - 1:xx * cy + cy]
            return 0

        lax.fori_loop(0, cx // add_x, add_chunk, 0)

    read_records(0)
    read_segments()
    for w in range(seg_tiles):
        seg[w] = seg_pre[w]

    def step(s, _):
        p = lax.rem(s, 2)
        after = jnp.minimum(s + 1, steps - 1)
        halos = (
            (a > 0, remote(D.at[:, 1, core], xh.at[p, 1], xe_send.at[0], xh_recv.at[p, 1], (a - 1, b)), 0),
            (a < n_gx - 1, remote(D.at[:, cx, core], xh.at[p, 0], xe_send.at[1], xh_recv.at[p, 0], (a + 1, b)), 1),
        )
        y_halos = (
            (b > 0, remote(ye.at[0], yh.at[p, 1], ye_send.at[0], yh_recv.at[p, 1], (a, b - 1)), 0),
            (b < n_gy - 1, remote(ye.at[1], yh.at[p, 0], ye_send.at[1], yh_recv.at[p, 0], (a, b + 1)), 1),
        )

        def wait_from(dst, recv):
            pltpu.make_async_copy(dst, dst, recv).wait()

        recs = [recs_buf[w] for w in range(rec_tiles)]
        for o in range(n_gy):
            idx = rows8(inv[s, o:o + 1, :])
            out = jnp.zeros((8, LANES), F32)
            for w in range(rec_tiles):
                out = jnp.where((idx >> 7) == w, take_lanes(recs[w], idx & 127), out)
            msg[o] = out
        rx[p, b] = msg[b]
        m_copies = []
        for k in range(1, n_gy):
            o = lax.rem(b + k, n_gy)
            m_copies.append(remote(msg.at[o], rx.at[p, b], m_send.at[k], m_recv.at[p, b], (a, o)))
            m_copies[-1].start()
        p_copy = remote(seg, ps.at[p], p_send, p_recv.at[p], (mate, b))
        p_copy.start()

        @pl.when(s > 0)
        def _():
            add_forces(s - 1)

        for there, copy, _k in halos + y_halos:
            @pl.when(there)
            def _(copy=copy):
                copy.start()

        goal = jnp.concatenate([cells_v[after, 0], contact_v[...] * LANES + (LANES - 1)], axis=1).astype(F32)

        def match_tile(w, _):
            at = pl.ds(pl.multiple_of(w * LANES, LANES), LANES)
            col = cell_col[s, at, :]
            for t in range(rec_tiles + seg_tiles):
                ts = slice(t * LANES, (t + 1) * LANES)
                match_hot[at, ts] = jnp.where(col == goal[:, ts], 1.0, 0.0).astype(BF16)
            return 0

        lax.fori_loop(0, rec_tiles, match_tile, 0)
        for j in range(n_blocks):
            state = part[j]
            idx = nbr[j]
            for f in range(6):
                near[j, f] = take_lanes(rows8(state[f:f + 1]), idx)

        wait_from(ps.at[p], p_recv.at[p])
        c_parts = [[], []]
        for w in range(seg_tiles):
            idx = rows8(match_v[:, w * LANES:(w + 1) * LANES])
            facing = jnp.zeros((8, LANES), F32)
            for u in range(seg_tiles):
                facing = jnp.where((idx >> 7) == u, take_lanes(ps[p, u], idx & 127), facing)
            own = seg[w]
            pull = (TIME_STEP * CONTACT_K) * (facing - own) / own[6:7]
            hi, lo = two_parts(pltpu.roll(jnp.where(sub < 3, pull, 0.0), 5, 0))
            c_parts[0].append(hi)
            c_parts[1].append(lo)
        zero_rows = jnp.zeros((LANES - 8, n_seg), F32)
        c_mat = jnp.concatenate(
            [zero_rows, jnp.concatenate(c_parts[0], axis=1), zero_rows, jnp.concatenate(c_parts[1], axis=1)], axis=0
        ).astype(BF16)

        half = n_cols // 2

        def top_chunk(i, _):
            at = pl.ds(pl.multiple_of(i * half, half), half)
            hot = seg_hot[at, :]
            both = dot_nt(hot, c_mat)
            top_add[at, :] = both[:, :LANES] + both[:, LANES:]
            return 0

        lax.fori_loop(0, n_cols // half, top_chunk, 0)

        @pl.when(a > 0)
        def _():
            wait_from(xh.at[p, 0], xh_recv.at[p, 0])

        @pl.when(a < n_gx - 1)
        def _():
            wait_from(xh.at[p, 1], xh_recv.at[p, 1])

        @pl.when(b > 0)
        def _():
            wait_from(yh.at[p, 0], yh_recv.at[p, 0])

        @pl.when(b < n_gy - 1)
        def _():
            wait_from(yh.at[p, 1], yh_recv.at[p, 1])

        D[:, 0, core] = xh[p, 0]
        D[:, cx + 1, core] = xh[p, 1]

        def y_rows(i, _):
            for u in range(8):
                x = i * 8 + u
                for f in range(3):
                    D[f, x + 1, pl.ds(7, 1), :] = yh[p, 0, f, pl.ds(x, 1), :]
                    D[f, x + 1, pl.ds(8 + cy, 1), :] = yh[p, 1, f, pl.ds(x, 1), :]
            return 0

        lax.fori_loop(0, cx // 8, y_rows, 0)

        lane_i = lax.broadcasted_iota(jnp.int32, (cy, LANES), 1)

        def lap_row(x):
            top = top_add[pl.ds(pl.multiple_of(x * cy, cy), cy), :]
            scale = A[x]
            for f in range(3):
                c = D[f, x + 1, core]
                lap = D[f, x, core] + D[f, x + 2, core] - 6.0 * c
                lap += D[f, x + 1, pl.ds(7, cy)] + D[f, x + 1, pl.ds(9, cy)]
                lap += jnp.where(lane_i == 0, 0.0, pltpu.roll(c, 1, 1))
                lap += jnp.where(lane_i == LANES - 1, 0.0, pltpu.roll(c, LANES - 1, 1))
                push = jnp.where(lane_i == LANES - 1, pltpu.roll(top, 2 - f, 1) if f < 2 else top, 0.0)
                v = V[f, x] + scale * lap + push
                V[f, x] = v
                base = pl.multiple_of(x * (cy * 8), cy * 8)
                flat[pl.ds(base + f, cy, stride=8), :] = c + TIME_STEP * v
                flat[pl.ds(base + 3 + f, cy, stride=8), :] = v

        def lap_rows(i, _):
            for u in range(4):
                lap_row(4 * i + u)
            return 0

        lax.fori_loop(0, cx // 16, lap_rows, 0)

        for k in range(1, n_gy):
            src = lax.rem(b + k, n_gy)
            wait_from(rx.at[p, src], m_recv.at[p, src])
        got = [rx[p, src] for src in range(n_gy)]
        replies = [jnp.zeros((8, LANES), F32) for _ in range(n_gy)]
        springs = []
        for j in range(n_blocks):
            rec = jnp.zeros((8, LANES), F32)
            for src in range(n_gy):
                moved = pltpu.roll(got[src], ((src - j) * group) % LANES, 1) if src != j else got[src]
                rec = jnp.where(lane // group == src, moved, rec)
            diff = [near[j, f] - rec[f:f + 1] for f in range(6)]
            gain = rec[6:7] / (1.0 + diff[0] * diff[0] + diff[1] * diff[1] + diff[2] * diff[2])
            force = jnp.zeros((8, LANES), F32)
            for f in range(3):
                spring = gain * (PARTICLE_K * diff[f])
                springs.append(spring)
                total = jnp.sum(spring + gain * (DRAG_COEF * diff[3 + f]), axis=0, keepdims=True)
                force = jnp.where(sub == f, total, force)
            force = force * (1.0 / n_nbr)
            for src in range(n_gy):
                moved = pltpu.roll(force, ((j - src) * group) % LANES, 1) if src != j else force
                replies[src] = jnp.where(lane // group == j, moved, replies[src])
        for src in range(n_gy):
            ans[src] = replies[src]
        ax[p, b] = ans[b]
        a_copies = []
        for k in range(1, n_gy):
            o = lax.rem(b + k, n_gy)
            a_copies.append(remote(ans.at[o], ax.at[p, b], a_send.at[k], a_recv.at[p, b], (a, o)))
            a_copies[-1].start()

        for j in range(n_blocks):
            parts = [two_parts(springs[3 * j + f]) for f in range(3)]
            lhs = jnp.concatenate([q[0] for q in parts] + [q[1] for q in parts], axis=0).astype(BF16)
            wide = jnp.dot(lhs, nbr_hot[j], preferred_element_type=F32)
            change = jnp.zeros((8, LANES), F32)
            for f in range(3):
                acc = jnp.zeros((8, LANES), F32)
                for k in range(n_nbr):
                    ks = slice(k * LANES, (k + 1) * LANES)
                    acc = jnp.where(sub == k, wide[8 * f:8 * f + 8, ks] + wide[24 + 8 * f:32 + 8 * f, ks], acc)
                total = jnp.sum(acc, axis=0, keepdims=True) * (-TIME_STEP / n_nbr)
                change = change + jnp.where(sub == 3 + f, total, 0.0)
            state = part[j] + change
            part[j] = state + jnp.where(sub < 3, TIME_STEP * pltpu.roll(state, 5, 0), 0.0)

        lax.fori_loop(cx // 16, cx // 4, lap_rows, 0)
        masses = [recs_buf[w, 6:7, :] for w in range(rec_tiles)]

        @pl.when(s < steps - 1)
        def _():
            read_records(after)
            read_segments()


        for k in range(1, n_gy):
            src = lax.rem(b + k, n_gy)
            wait_from(ax.at[p, src], a_recv.at[p, src])
        own_row = owner_v[s, 0]
        rank_row = rank[pl.ds(s, 1), :]
        rows = []
        for w in range(rec_tiles):
            ws = slice(w * LANES, (w + 1) * LANES)
            own8, rank8 = rows8(own_row[:, ws]), rows8(rank_row[:, ws])
            force = jnp.zeros((8, LANES), F32)
            for o in range(n_gy):
                force = jnp.where(own8 == o, take_lanes(ax[p, o], rank8), force)
            hi, lo = two_parts(TIME_STEP * force / masses[w])
            push_buf[0, w] = hi
            push_buf[1, w] = lo
            rows.append(jnp.concatenate([hi, lo], axis=0))
        both = jnp.dot(jnp.concatenate(rows, axis=1).astype(BF16), match_hot[...], preferred_element_type=F32)
        more = both[:8] + both[8:]
        more = TIME_STEP * more + pltpu.roll(more, 3, 0)
        for copy in m_copies + a_copies + [p_copy]:
            copy.wait_send()
        for there, copy, _k in halos + y_halos:
            @pl.when(there)
            def _(copy=copy):
                copy.wait_send()
        for w in range(rec_tiles):
            recs_buf[w] = recs_buf[w] + more[:, w * LANES:(w + 1) * LANES]
        for w in range(seg_tiles):
            seg[w] = seg_pre[w] + more[:, n_rec + w * LANES:n_rec + (w + 1) * LANES]
        return 0

    lax.fori_loop(0, steps, step, 0)
    add_forces(steps - 1)
    out_d = pltpu.make_async_copy(D.at[:, pl.ds(1, cx), core], disp_out, out_sem.at[0])
    out_v = pltpu.make_async_copy(V, vel_out, out_sem.at[1])
    out_d.start()
    out_v.start()
    out_d.wait()
    out_v.wait()


def local(n_gx, n_gy, disp, vel, stiff, mass, contact_cells, contact_match, eroded, owners, bpos, bvel, bnbr):
    cx, cy, nz = disp.shape[1:]
    steps, n_rec = eroded.shape[0], eroded.shape[3]
    n_seg = contact_cells.shape[2]
    n_slots = bpos.shape[3]
    n_blocks = n_slots // LANES
    n_nbr = bnbr.shape[2]
    dims = (n_gx, n_gy, cx, cy, steps, n_rec, n_seg, n_blocks, n_nbr)
    contact = contact_cells.reshape(1, n_seg)
    cells = eroded.reshape(steps, 1, 1, n_rec)
    vm = pl.BlockSpec(memory_space=pltpu.VMEM)
    sm = pl.BlockSpec(memory_space=pltpu.SMEM)
    anywhere = pl.BlockSpec(memory_space=pl.ANY)
    dma = pltpu.SemaphoreType.DMA
    tile = (8, LANES)
    return pl.pallas_call(
        functools.partial(kernel, dims),
        out_shape=(jax.ShapeDtypeStruct(disp.shape, F32), jax.ShapeDtypeStruct(vel.shape, F32)),
        in_specs=[sm, sm] + [anywhere] * 4 + [vm] * 7,
        out_specs=(anywhere, anywhere),
        scratch_shapes=[
            pltpu.VMEM((3, cx + 2, cy + 16, nz), F32),
            pltpu.VMEM((3, cx, cy, nz), F32),
            pltpu.VMEM((cx, cy, nz), F32),
            pltpu.VMEM((cx, cy, nz), F32),
            pltpu.VMEM((cx * cy, 8, nz), F32),
            pltpu.VMEM((n_rec // LANES,) + tile, F32),
            pltpu.VMEM((n_seg // LANES,) + tile, F32),
            pltpu.VMEM((2, n_rec // LANES) + tile, F32),
            pltpu.VMEM((n_blocks, 6) + tile, F32),
            pltpu.VMEM((n_rec, n_rec + n_seg), BF16),
            pltpu.VMEM((steps, n_rec, LANES), F32),
            pltpu.VMEM((cx * cy, nz), F32),
            pltpu.VMEM((2, 3, cx, nz), F32),
            pltpu.VMEM((2, 2, 3, cx, nz), F32),
            pltpu.VMEM((2, 2, 3, cy, nz), F32),
            pltpu.VMEM((n_gy,) + tile, F32),
            pltpu.VMEM((2, n_gy) + tile, F32),
            pltpu.VMEM((n_gy,) + tile, F32),
            pltpu.VMEM((2, n_gy) + tile, F32),
            pltpu.VMEM((n_seg // LANES,) + tile, F32),
            pltpu.VMEM((2, n_seg // LANES) + tile, F32),
            pltpu.VMEM((steps, n_gy, LANES), jnp.int32),
            pltpu.VMEM((steps, n_rec), jnp.int32),
            pltpu.VMEM((n_blocks,) + tile, F32),
            pltpu.VMEM((n_blocks,) + tile, jnp.int32),
            pltpu.VMEM((n_blocks, LANES, n_nbr * LANES), BF16),
            pltpu.VMEM((cx * cy, n_seg), BF16),
            pltpu.VMEM((6 * LANES, n_rec), BF16),
            dma((2,)), dma((4,)),
            dma((2,)), dma((2, 2)),
            dma((2,)), dma((2, 2)),
            dma((n_gy,)), dma((2, n_gy)),
            dma((n_gy,)), dma((2, n_gy)),
            dma, dma((2,)),
        ],
        compiler_params=pltpu.CompilerParams(collective_id=0, has_side_effects=True, vmem_limit_bytes=60 * 2**20),
        name="dynamics",
    )(
        cells, contact, disp, vel, stiff, mass, contact, contact_match.reshape(1, n_seg), cells,
        owners.reshape(steps, 1, 1, n_rec), bpos.transpose(2, 0, 1, 3), bvel.transpose(2, 0, 1, 3), bnbr,
    )


def solution(mesh):
    return jax.shard_map(
        functools.partial(local, mesh.shape["gx"], mesh.shape["gy"]),
        mesh=mesh,
        in_specs=(
            P(None, "gx", "gy", None),
            P(None, "gx", "gy", None),
            P("gx", "gy", None),
            P("gx", "gy", None),
            P("gx", "gy", None),
            P("gx", "gy", None),
            P(None, "gx", "gy", None),
            P(None, "gx", "gy", None, None),
            P("gx", "gy", None, None),
            P("gx", "gy", None, None),
            P("gx", "gy", None, None),
        ),
        out_specs=(P(None, "gx", "gy", None), P(None, "gx", "gy", None)),
        check_vma=False,
    )
```
